32 devices in a mesh: groups: 2 (over y), probe: 4 (over z), depth: 2 (over x), tile: 2 (over core).
Axes of the slice: x: 2, y: 2, z: 4, core: 2. Of those that a mesh axis runs over, the one named last changes fastest.
Arguments:
- stored_waves: bfloat16 [2, 16, 2, 256, 256], P('depth', ('groups', 'probe', 'tile')), parts along dimension 1, may hold values from -6 to 6
- transmission: bfloat16 [2, 16, 2, 256, 256], P('depth', ('groups', 'probe', 'tile')), parts along dimension 1
- residual: float32 [16, 2, 256, 256], P(('groups', 'probe', 'tile')), parts along dimension 0, may hold values from -0.6 to 0.6
- offsets: int32 [16, 2], P('groups'), parts along dimension 0, may hold values from 0 to 256
- slot_position: int32 [16], P(('groups', 'probe', 'tile')), parts along dimension 0, may hold values from 0 to 7, each once
Outputs:
- object_gradient: float32 [4, 2, 512, 512], P('groups', 'depth', 'probe', 'tile'), parts along dimension 0
The draws below stay inside these ranges and needn't reach their ends.
There are 2 independent parts, one for each index of `groups`. The reference program is written for one: setup_inputs(seed, part) draws one part's arguments, and reference() takes and returns one part's arrays. A program takes and returns all parts, laid end to end along the dimension named above; each array names one. Nothing has to cross between parts.
Inputs may be any that keep to these rules, and one draw needn't show every extreme that they name: `slot_position`: every scan position is held by exactly one slot.
All inputs are finite; a program needn't handle non-finite values.
Results may differ from the reference program's by a relative error of at most 0.0032.
Values may be sent and summed in bfloat16 or wider, within the bound.
No kernel may reach another device: no remote copies, remote signals or barrier semaphores. Data moves between devices by JAX's collectives and lax.ppermute only.
A program may use at most 64 MiB of HBM per device.

```python
import math
import jax
import jax.numpy as jnp
from jax import lax

W = 256
OBJ = 512
SLICES = 2
POSITIONS = 8


def draw_transmission(key, part):
    amp_key, phase_key = jax.random.split(key)
    draw_shape = (SLICES, POSITIONS, 1, W, W)
    amplitude = jnp.exp(jax.random.uniform(amp_key, draw_shape, jnp.float32, math.log(0.75), 0.0))
    phase_angle = jax.random.uniform(phase_key, draw_shape, jnp.float32, -math.pi, math.pi)
    return jnp.concatenate([amplitude * jnp.cos(phase_angle), amplitude * jnp.sin(phase_angle)], axis=2).astype(jnp.bfloat16)


def set_ends(values, own_key, least, largest):
    place = [jax.random.randint(jax.random.fold_in(own_key, axis), (), 0, length) for axis, length in enumerate(values.shape)]
    main_axis = values.shape.index(max(values.shape))
    next_to = place[:main_axis] + [(place[main_axis] + 1) % values.shape[main_axis]] + place[main_axis + 1:]
    return values.at[tuple(place)].set(least).at[tuple(next_to)].set(largest)


def block_scale(stream_key, dims, cuts, smallest, top_value):
    def one(axis_at, shards_of):
        draws = jax.random.uniform(jax.random.fold_in(jax.random.fold_in(stream_key, 6), axis_at), (shards_of,), jnp.float32, smallest / len(cuts), top_value / len(cuts))
        return jnp.repeat(jnp.exp(draws), dims[axis_at] // shards_of).reshape((-1,) + (1,) * (len(dims) - axis_at - 1))

    level = one(*cuts[0])
    for cut in cuts[1:]:
        level = level * one(*cut)
    return level


def centred(rng, shape, scale, reach, cuts=(), kind=jnp.bfloat16):
    values = jax.random.normal(rng, shape, jnp.float32) * scale
    if len(cuts) > 0:
        values = block_scale(rng, shape, cuts, -0.22, 0.18) * values
    return jnp.clip(values, min=-reach, max=reach).astype(kind)


def setup_inputs(seed: int = 0, part: int = 0) -> dict:
    keys = jax.random.split(jax.random.key(seed), 6)
    own_keys = jax.random.split(jax.random.fold_in(keys[5], part), 6)
    stored_waves = centred(own_keys[0], (SLICES, POSITIONS, 2, W, W), 1.0, 6.0, ((0, 2), (1, 8)))
    transmission = draw_transmission(jax.random.fold_in(jax.random.fold_in(keys[5], part), 71), part)
    residual = centred(own_keys[2], (POSITIONS, 2, W, W), 0.1, 0.6, ((0, 8),), jnp.float32)
    offsets = set_ends(jax.random.randint(own_keys[3], (POSITIONS, 2), 0, OBJ - W + 1), jax.random.fold_in(own_keys[3], 1), 0, OBJ - W).astype(jnp.int32)
    slot_position = jax.random.permutation(own_keys[4], POSITIONS).astype(jnp.int32)
    return dict(stored_waves=stored_waves, transmission=transmission, residual=residual, offsets=offsets, slot_position=slot_position)


def back_propagate(field_real, field_imag):
    side_length = field_real.shape[-1]
    counter = jnp.arange(side_length, dtype=jnp.int32)
    frequency = ((counter + side_length // 2) % side_length - side_length // 2).astype(jnp.float32)
    phase_angle = 0.5 * (frequency[:, None] * frequency[:, None] + frequency[None, :] * frequency[None, :]) / side_length
    spectrum = jnp.fft.fft2(field_real + 1j * field_imag)
    spectrum = spectrum * (jnp.cos(phase_angle) + 1j * jnp.sin(phase_angle))
    result = jnp.fft.ifft2(spectrum)
    return jnp.real(result), jnp.imag(result)


def reference(stored_waves, transmission, residual, offsets, slot_position):
    slice_count = stored_waves.shape[0]
    positions = stored_waves.shape[1]
    side_length = stored_waves.shape[-1]
    corners = offsets[slot_position]
    adjoint_real = residual[:, 0]
    adjoint_imag = residual[:, 1]
    handed_real = adjoint_real
    handed_imag = adjoint_imag
    grads_real = []
    grads_imag = []
    for slice_number in range(slice_count - 1, -1, -1):
        if slice_number < slice_count - 1:
            adjoint_real, adjoint_imag = back_propagate(handed_real, handed_imag)
        wave_real = stored_waves[slice_number, :, 0].astype(jnp.float32)
        wave_imag = stored_waves[slice_number, :, 1].astype(jnp.float32)
        grads_real.insert(0, wave_real * adjoint_real + wave_imag * adjoint_imag)
        grads_imag.insert(0, wave_real * adjoint_imag - wave_imag * adjoint_real)
        trans_real = transmission[slice_number, :, 0].astype(jnp.float32)
        trans_imag = transmission[slice_number, :, 1].astype(jnp.float32)
        rounded = lax.optimization_barrier(((trans_real * adjoint_real + trans_imag * adjoint_imag).astype(jnp.bfloat16),
                                            (trans_real * adjoint_imag - trans_imag * adjoint_real).astype(jnp.bfloat16)))
        handed_real = rounded[0].astype(jnp.float32)
        handed_imag = rounded[1].astype(jnp.float32)
    gradient = jnp.stack([jnp.stack(grads_real), jnp.stack(grads_imag)])
    region = jnp.zeros((2, slice_count, OBJ, OBJ), jnp.float32)

    def add_patch(number, region):
        patch_value = lax.dynamic_index_in_dim(gradient, number, 2, keepdims=False)
        anchor = jnp.int32(0)
        corner = (anchor, anchor, corners[number, 0].astype(jnp.int32), corners[number, 1].astype(jnp.int32))
        current = lax.dynamic_slice(region, corner, (2, slice_count, side_length, side_length))
        return lax.dynamic_update_slice(region, current + patch_value, corner)

    return lax.fori_loop(0, positions, add_patch, region)
```

```python
import functools
import math

import jax
import jax.numpy as jnp
import numpy as np
from jax import lax
from jax.experimental import pallas as pl
from jax.experimental.pallas import tpu as pltpu
from jax.sharding import PartitionSpec as P

OBJ = 512
TAIL = 16


def propagator(side):
    counter = np.arange(side)
    frequency = (counter + side // 2) % side - side // 2
    chirp = np.exp(0.5j * frequency.astype(np.float64) ** 2 / side)
    ring = np.fft.ifft(chirp)
    ring = 0.5 * (ring + ring[(-counter) % side])
    matrix = ring[(counter[:, None] - counter[None, :]) % side]
    parts = np.stack([matrix.real, matrix.imag]).astype(np.float32)
    high = parts.astype(jnp.bfloat16)
    low = (parts - high.astype(np.float32)).astype(jnp.bfloat16)
    return np.concatenate([high[0], high[1], low[0], low[1]], axis=0)


def mm(a, b):
    return jnp.dot(a, b, preferred_element_type=jnp.float32)


def split(x):
    high = x.astype(jnp.bfloat16)
    return high, (x - high.astype(jnp.float32)).astype(jnp.bfloat16)


def send_kernel(
    slot_ref, offsets_ref, table_ref, waves_ref, layer_ref, residual_ref,
    adj_own_ref, adj_other_ref, wave_own_ref, wave_other_ref, adj_ref, wave_ref,
):
    side = waves_ref.shape[-1]
    half = side // 2
    top = lax.axis_index("depth") == 1
    parity = lax.rem(lax.axis_index("probe"), 2)
    slot = slot_ref[0]
    cy, cx = offsets_ref[slot, 0], offsets_ref[slot, 1]
    rows = lax.broadcasted_iota(jnp.int32, (side, side), 0)
    cols = lax.broadcasted_iota(jnp.int32, (side, side), 1)
    roll_rows = (cols == ((rows - cy) & (side - 1))).astype(jnp.bfloat16)
    roll_cols = (rows == ((cols - cx) & (side - 1))).astype(jnp.bfloat16)

    def rolled(stacked):
        moved = mm(stacked, roll_cols).astype(jnp.bfloat16)
        return [
            mm(roll_rows, moved[n * side : (n + 1) * side]).astype(jnp.bfloat16)
            for n in range(stacked.shape[0] // side)
        ]

    @pl.when(top)
    def _():
        res_r, res_i = residual_ref[0], residual_ref[1]
        lay_r, lay_i = layer_ref[0].astype(jnp.float32), layer_ref[1].astype(jnp.float32)
        wav_r, wav_i = waves_ref[0].astype(jnp.float32), waves_ref[1].astype(jnp.float32)
        handed_r = (lay_r * res_r + lay_i * res_i).astype(jnp.bfloat16)
        handed_i = (lay_r * res_i - lay_i * res_r).astype(jnp.bfloat16)
        grad_r = (wav_r * res_r + wav_i * res_i).astype(jnp.bfloat16)
        grad_i = (wav_r * res_i - wav_i * res_r).astype(jnp.bfloat16)
        hr, hi, gr, gi = rolled(jnp.concatenate([handed_r, handed_i, grad_r, grad_i], axis=0))
        wave_ref[0] = gr
        wave_ref[1] = gi
        handed = jnp.concatenate([hr, hi], axis=0)
        tables = [table_ref[n * side : (n + 1) * side] for n in range(4)]
        by_r = mm(handed, tables[2]) + mm(handed, tables[0])
        by_i = mm(handed, tables[3]) + mm(handed, tables[1])
        mid_r = by_r[:side] - by_i[side:]
        mid_i = by_r[side:] + by_i[:side]
        mrh, mrl = split(mid_r)
        mih, mil = split(mid_i)
        tall, short = table_ref[...], table_ref[: 2 * side]
        hi_r, hi_i = mm(tall, mrh), mm(tall, mih)
        lo_r, lo_i = mm(short, mrl), mm(short, mil)
        rr = hi_r[:side] + (hi_r[2 * side : 3 * side] + lo_r[:side])
        ir = hi_r[side : 2 * side] + (hi_r[3 * side :] + lo_r[side:])
        ri = hi_i[:side] + (hi_i[2 * side : 3 * side] + lo_i[:side])
        ii = hi_i[side : 2 * side] + (hi_i[3 * side :] + lo_i[side:])
        adj_ref[0] = (rr - ii).astype(jnp.bfloat16)
        adj_ref[1] = (ri + ir).astype(jnp.bfloat16)

    @pl.when(jnp.logical_not(top))
    def _():
        wr, wi = rolled(jnp.concatenate([waves_ref[0], waves_ref[1]], axis=0))
        wave_ref[0] = wr
        wave_ref[1] = wi
        adj_ref[...] = jnp.zeros_like(adj_ref)

    line = lax.broadcasted_iota(jnp.int32, (TAIL, side), 0)
    tail = jnp.where(line == 0, cy.astype(jnp.float32), cx.astype(jnp.float32)).astype(jnp.bfloat16)
    own = pl.ds(pl.multiple_of(parity * half, half), half)
    other = pl.ds(pl.multiple_of((1 - parity) * half, half), half)
    adj_own_ref[...] = adj_ref[:, own]
    adj_other_ref[...] = adj_ref[:, other]
    wave_own_ref[:, :half] = wave_ref[:, own]
    wave_other_ref[:, :half] = wave_ref[:, other]
    for part in range(2):
        wave_own_ref[part, half:] = tail
        wave_other_ref[part, half:] = tail


def gather_kernel(w0, w1, w2, w3, a0, a1, a2, a3, keep_ref, send_ref):
    half, side = a0.shape[1], a0.shape[2]
    place = lax.axis_index("probe")
    top = lax.axis_index("depth") == 1
    upper = place >= 2
    right = lax.axis_index("tile") == 1
    parity = lax.rem(place, 2)
    rows = (lax.broadcasted_iota(jnp.int32, (half, side), 0) + parity * half).astype(jnp.float32)
    cols = lax.broadcasted_iota(jnp.int32, (half, side), 1).astype(jnp.float32)
    keep = [jnp.zeros((half, side), jnp.float32)] * 2
    send = [jnp.zeros((half, side), jnp.float32)] * 2
    zero = jnp.zeros((half, side), jnp.float32)
    for w, a in ((w0, a0), (w1, a1), (w2, a2), (w3, a3)):
        tail = w[0, half:].astype(jnp.float32)
        cy, cx = tail[0:1], tail[1:2]
        wr, wi = w[0, :half].astype(jnp.float32), w[1, :half].astype(jnp.float32)
        ar, ai = a[0].astype(jnp.float32), a[1].astype(jnp.float32)
        here = (cols < cx) == right
        mine = (rows < cy) == upper
        gr = jnp.where(here, jnp.where(top, wr, wr * ar + wi * ai), zero)
        gi = jnp.where(here, jnp.where(top, wi, wr * ai - wi * ar), zero)
        keep = [keep[0] + jnp.where(mine, gr, zero), keep[1] + jnp.where(mine, gi, zero)]
        send = [send[0] + jnp.where(mine, zero, gr), send[1] + jnp.where(mine, zero, gi)]
    for part in range(2):
        keep_ref[part] = keep[part]
        send_ref[part] = send[part].astype(jnp.bfloat16)


def two_slices(stored_waves, transmission, residual, offsets, slot_position):
    side = stored_waves.shape[-1]
    half = side // 2
    table = jnp.asarray(propagator(side))
    vmem, smem = (pl.BlockSpec(memory_space=m) for m in (pltpu.VMEM, pltpu.SMEM))
    block = jax.ShapeDtypeStruct((2, half, side), jnp.bfloat16)
    tailed = jax.ShapeDtypeStruct((2, half + TAIL, side), jnp.bfloat16)
    adj_own, adj_other, wave_own, wave_other = pl.pallas_call(
        send_kernel,
        out_shape=(block, block, tailed, tailed),
        in_specs=[smem, smem, vmem, vmem, vmem, vmem],
        out_specs=(vmem,) * 4,
        scratch_shapes=[pltpu.VMEM((2, side, side), jnp.bfloat16)] * 2,
        compiler_params=pltpu.CompilerParams(vmem_limit_bytes=32 * 1024 * 1024),
        name="adjoint_and_rolls",
    )(slot_position, offsets, table, stored_waves[0, 0], transmission[0, 0], residual[0])

    probe_count = lax.axis_size("probe")
    swap_tile = [(0, 1), (1, 0)]
    flip = [(2 * z + d, 2 * z + 1 - d) for z in range(probe_count) for d in range(2)]
    flip_z1 = [(2 * z + d, 2 * (z ^ 1) + 1 - d) for z in range(probe_count) for d in range(2)]
    z1 = [(z, z ^ 1) for z in range(probe_count)]
    z2 = [(z, z ^ 2) for z in range(probe_count)]
    a_own = lax.ppermute(adj_own, ("probe", "depth"), flip)
    a_next = lax.ppermute(adj_other, ("probe", "depth"), flip_z1)
    w_next = lax.ppermute(wave_other, "probe", z1)
    w_side = lax.ppermute(wave_own, "tile", swap_tile)
    a_side = lax.ppermute(a_own, "tile", swap_tile)
    w_next_side = lax.ppermute(w_next, "tile", swap_tile)
    a_next_side = lax.ppermute(a_next, "tile", swap_tile)
    keep, send = pl.pallas_call(
        gather_kernel,
        out_shape=(jax.ShapeDtypeStruct((2, half, side), jnp.float32), block),
        in_specs=[vmem] * 8,
        out_specs=(vmem,) * 2,
        compiler_params=pltpu.CompilerParams(vmem_limit_bytes=32 * 1024 * 1024),
        name="masked_sums",
    )(wave_own, w_side, w_next, w_next_side, a_own, a_side, a_next, a_next_side)
    got = lax.ppermute(send, "probe", z2)
    return (keep + got.astype(jnp.float32))[:, None]


def times(a, b, spec):
    return jnp.einsum(spec, a, b, precision=lax.Precision.HIGHEST)


def back_propagate(field):
    side = field.shape[-1]
    table = jnp.asarray(propagator(side)).astype(jnp.float32).reshape(2, 2, side, side)
    real, imag = table[0] + table[1]
    for spec in ("kn,pnm->pkm", "mk,pnm->pnk"):
        fr, fi = field[:, 0], field[:, 1]
        field = jnp.stack(
            [times(real, fr, spec) - times(imag, fi, spec), times(real, fi, spec) + times(imag, fr, spec)], 1
        )
    return field


def any_slices(stored_waves, transmission, residual, offsets, slot_position):
    slot_count, side = stored_waves.shape[1], stored_waves.shape[-1]
    depth_count, depth_index = lax.axis_size("depth"), lax.axis_index("depth")
    waves = stored_waves[0].astype(jnp.float32)
    layers = transmission[0].astype(jnp.float32)

    def conj_times(a, b):
        return jnp.stack([a[:, 0] * b[:, 0] + a[:, 1] * b[:, 1], a[:, 0] * b[:, 1] - a[:, 1] * b[:, 0]], 1)

    adjoint = residual
    for turn in range(1, depth_count):
        handed = conj_times(layers, adjoint).astype(jnp.bfloat16)
        got = lax.ppermute(handed, "depth", [(d, d - 1) for d in range(1, depth_count)])
        active = depth_index == depth_count - 1 - turn
        adjoint = lax.cond(active, lambda: back_propagate(got.astype(jnp.float32)), lambda: adjoint)
    gradient = jnp.moveaxis(conj_times(waves, adjoint), 1, 0)
    corners = offsets[slot_position]

    def add_patch(number, region):
        patch = lax.dynamic_index_in_dim(gradient, number, 1, keepdims=True)
        corner = (0, 0, corners[number, 0], corners[number, 1])
        current = lax.dynamic_slice(region, corner, patch.shape)
        return lax.dynamic_update_slice(region, current + patch, corner)

    region = lax.fori_loop(0, slot_count, add_patch, jnp.zeros((2, 1, OBJ, OBJ), jnp.float32))
    strips = lax.psum_scatter(region, "probe", scatter_dimension=2, tiled=True)
    return lax.psum_scatter(strips, "tile", scatter_dimension=3, tiled=True)


def solution(mesh):
    sizes = dict(mesh.shape)

    def per_device(stored_waves, *rest):
        small = (sizes["depth"], sizes["probe"], sizes["tile"], stored_waves.shape[1]) == (2, 4, 2, 1)
        return (two_slices if small else any_slices)(stored_waves, *rest)

    slots = ("groups", "probe", "tile")
    return jax.shard_map(
        per_device,
        mesh=mesh,
        in_specs=(
            P("depth", slots, None, None, None),
            P("depth", slots, None, None, None),
            P(slots, None, None, None),
            P("groups", None),
            P(slots),
        ),
        out_specs=P("groups", "depth", "probe", "tile"),
        check_vma=False,
    )
```

```python
import functools
import math

import jax
import jax.numpy as jnp
import numpy as np
from jax import lax
from jax.experimental import pallas as pl
from jax.experimental.pallas import tpu as pltpu
from jax.sharding import PartitionSpec as P

OBJ = 512
TAIL = 16


def propagator(side):
    counter = np.arange(side)
    frequency = (counter + side // 2) % side - side // 2
    chirp = np.exp(0.5j * frequency.astype(np.float64) ** 2 / side)
    ring = np.fft.ifft(chirp)
    ring = 0.5 * (ring + ring[(-counter) % side])
    matrix = ring[(counter[:, None] - counter[None, :]) % side]
    return np.stack([matrix.real, matrix.imag]).astype(np.float32)


def mm(a, b):
    return jnp.dot(a, b, preferred_element_type=jnp.float32)


def split(x):
    high = x.astype(jnp.bfloat16)
    return high, (x - high.astype(jnp.float32)).astype(jnp.bfloat16)


def rolls(side, cy, cx):
    down = lax.broadcasted_iota(jnp.int32, (side, side), 0)
    along = lax.broadcasted_iota(jnp.int32, (side, side), 1)
    rows = (along == ((down - cy) & (side - 1))).astype(jnp.bfloat16)
    cols = (down == ((along - cx) & (side - 1))).astype(jnp.bfloat16)
    return rows, cols


def rolled(parts, rows, cols):
    side = rows.shape[0]
    moved = mm(jnp.concatenate(parts, axis=0), cols).astype(jnp.bfloat16)
    return [mm(rows, moved[n * side : (n + 1) * side]).astype(jnp.bfloat16) for n in range(len(parts))]


def conj_times(a, b):
    return a[0] * b[0] + a[1] * b[1], a[0] * b[1] - a[1] * b[0]


def own_and_other(half):
    parity = lax.rem(lax.axis_index("probe"), 2)
    return (pl.ds(pl.multiple_of(n * half, half), half) for n in (parity, 1 - parity))


def send_kernel(
    slot_ref, offsets_hbm, table_hbm, layer_hbm, residual_hbm,
    own_ref, other_ref,
    offsets_ref, table_ref, layer_ref, residual_ref, sems,
):
    side = layer_ref.shape[-1]
    half = side // 2
    pairs = (
        (offsets_hbm, offsets_ref), (table_hbm, table_ref), (layer_hbm, layer_ref), (residual_hbm, residual_ref),
    )
    offsets_copy, table_copy, layer_copy, residual_copy = copies = [
        pltpu.make_async_copy(source, target, sems.at[n]) for n, (source, target) in enumerate(pairs)
    ]
    for copy in copies:
        copy.start()
    offsets_copy.wait()
    slot = slot_ref[0]
    cy, cx = offsets_ref[0, slot], offsets_ref[1, slot]
    parity = lax.rem(lax.axis_index("probe"), 2)
    down = (cy - parity * half) & (side - 1)
    line = lax.broadcasted_iota(jnp.int32, (TAIL, side), 0)
    tail = jnp.where(line == 0, cy.astype(jnp.float32), cx.astype(jnp.float32)).astype(jnp.bfloat16)
    own_ref[2 * half :] = tail
    other_ref[2 * half :] = tail
    top = lax.axis_index("depth") == 1

    def put(part, x):
        own_ref[part * half : (part + 1) * half] = x[:half]
        other_ref[part * half : (part + 1) * half] = x[half:]

    @pl.when(top)
    def _():
        table_copy.wait()
        (rhr, rlr), (rhi, rli) = (split(pltpu.roll(table_ref[n], cx, 1)) for n in range(2))
        (lhr, llr), (lhi, lli) = (split(pltpu.roll(table_ref[n], (side - down) & (side - 1), 1)) for n in range(2))
        layer_copy.wait()
        residual_copy.wait()
        layer = layer_ref[0].astype(jnp.float32), layer_ref[1].astype(jnp.float32)
        handed = conj_times(layer, (residual_ref[0], residual_ref[1]))
        vr, vi = (x.astype(jnp.bfloat16) for x in handed)
        field = jnp.concatenate([vr, vr, vi, vi], axis=1)
        middle = (
            mm(field, jnp.concatenate([rlr, rhr, -rli, -rhi], axis=0)),
            mm(field, jnp.concatenate([rli, rhi, rlr, rhr], axis=0)),
        )
        (mhr, mlr), (mhi, mli) = map(split, middle)
        field = jnp.concatenate([mlr, mhr, mhr, mli, mhi, mhi], axis=0)
        for part, x in enumerate(([lhr, llr, lhr, -lhi, -lli, -lhi], [lhi, lli, lhi, lhr, llr, lhr])):
            put(part, mm(jnp.concatenate(x, axis=1), field).astype(jnp.bfloat16))

    @pl.when(jnp.logical_not(top))
    def _():
        for copy in (layer_copy, residual_copy, table_copy):
            copy.wait()
        rows, cols = rolls(side, down, cx)
        for part, x in enumerate(rolled([residual_ref[n].astype(jnp.bfloat16) for n in range(2)], rows, cols)):
            put(part, x)


def sums_kernel(a0, a1, w0, w1, keep_ref, send_ref, side_keep_ref, side_send_ref):
    side = w0.shape[-1]
    half = side // 2
    place = lax.axis_index("probe")
    upper = place >= 2
    right = lax.axis_index("tile") == 1
    parity = lax.rem(place, 2)
    down = lax.broadcasted_iota(jnp.int32, (half, side), 0) + parity * half
    along = lax.broadcasted_iota(jnp.int32, (half, side), 1)
    every = lax.broadcasted_iota(jnp.int32, (side, side), 0)
    across = lax.broadcasted_iota(jnp.int32, (side, side), 1)
    zero = jnp.zeros((half, side), jnp.float32)
    slots = []
    for w, a in ((w0, a0), (w1, a1)):
        tail = a[2 * half :].astype(jnp.float32)
        cy, cx = tail[0:1].astype(jnp.int32), tail[1:2].astype(jnp.int32)
        rows = (along == ((down - cy) & (side - 1))).astype(jnp.bfloat16)
        cols = (every == ((across - cx) & (side - 1))).astype(jnp.bfloat16)
        moved = mm(rows, jnp.concatenate([w[0], w[1]], axis=1)).astype(jnp.bfloat16)
        moved = mm(jnp.concatenate([moved[:, :side], moved[:, side:]], axis=0), cols)
        wave = moved[:half], moved[half:]
        adjoint = a[:half].astype(jnp.float32), a[half : 2 * half].astype(jnp.float32)
        slots.append((conj_times(wave, adjoint), (down < cy) == upper, (along < cx) == right))
    for part in range(2):
        for ref, near, here in (
            (keep_ref, True, True), (send_ref, False, True), (side_keep_ref, True, False), (side_send_ref, False, False),
        ):
            total = zero
            for gradient, mine, own in slots:
                chosen = jnp.logical_and(mine if near else ~mine, own if here else ~own)
                total = total + jnp.where(chosen, gradient[part], zero)
            ref[part] = total.astype(ref.dtype)


def in_hbm(*arrays):
    return [pltpu.with_memory_space_constraint(x, pltpu.HBM) for x in arrays]


def two_slices(stored_waves, transmission, residual, offsets, slot_position):
    side = stored_waves.shape[-1]
    half = side // 2
    table = jnp.asarray(propagator(side))
    vmem, smem, hbm = (pl.BlockSpec(memory_space=m) for m in (pltpu.VMEM, pltpu.SMEM, pltpu.HBM))
    block, sums = (jax.ShapeDtypeStruct((2, half, side), t) for t in (jnp.bfloat16, jnp.float32))
    tailed = jax.ShapeDtypeStruct((2 * half + TAIL, side), jnp.bfloat16)
    params = pltpu.CompilerParams(vmem_limit_bytes=32 * 1024 * 1024)
    by_column = offsets.T
    waves = stored_waves[0, 0]
    adj_own, adj_other = pl.pallas_call(
        send_kernel,
        out_shape=(tailed, tailed),
        in_specs=[smem] + [hbm] * 4,
        out_specs=(vmem,) * 2,
        scratch_shapes=[
            pltpu.SMEM(by_column.shape, jnp.int32),
            pltpu.VMEM(table.shape, jnp.float32),
            pltpu.VMEM((2, side, side), jnp.bfloat16),
            pltpu.VMEM((2, side, side), jnp.float32),
            pltpu.SemaphoreType.DMA((4,)),
        ],
        compiler_params=params,
        name="adjoint",
    )(slot_position, *in_hbm(by_column, table, transmission[0, 0], residual[0]))

    probe_count = lax.axis_size("probe")
    swap_tile = [(0, 1), (1, 0)]
    flip = [(2 * z + d, 2 * z + 1 - d) for z in range(probe_count) for d in range(2)]
    flip_z1 = [(2 * z + d, 2 * (z ^ 1) + 1 - d) for z in range(probe_count) for d in range(2)]
    z1 = [(z, z ^ 1) for z in range(probe_count)]
    z2 = [(z, z ^ 2) for z in range(probe_count)]
    a_own = lax.ppermute(adj_own, ("probe", "depth"), flip)
    a_next = lax.ppermute(adj_other, ("probe", "depth"), flip_z1)
    w_next = lax.ppermute(waves, "probe", z1)
    keep, send, side_keep, side_send = pl.pallas_call(
        sums_kernel,
        out_shape=(sums, sums, block, block),
        in_specs=[vmem] * 4,
        out_specs=(vmem,) * 4,
        compiler_params=params,
        name="masked_sums",
    )(a_own, a_next, waves, w_next)
    send = send + lax.ppermute(side_send, "tile", swap_tile).astype(jnp.float32)
    got = lax.ppermute(send.astype(jnp.bfloat16), "probe", z2)
    keep = keep + lax.ppermute(side_keep, "tile", swap_tile).astype(jnp.float32)
    return (keep + got.astype(jnp.float32))[:, None]


def times(a, b, spec):
    return jnp.einsum(spec, a, b, precision=lax.Precision.HIGHEST)


def back_propagate(field):
    side = field.shape[-1]
    real, imag = jnp.asarray(propagator(side))
    for spec in ("kn,pnm->pkm", "mk,pnm->pnk"):
        fr, fi = field[:, 0], field[:, 1]
        field = jnp.stack(
            [times(real, fr, spec) - times(imag, fi, spec), times(real, fi, spec) + times(imag, fr, spec)], 1
        )
    return field


def any_slices(stored_waves, transmission, residual, offsets, slot_position):
    slot_count, side = stored_waves.shape[1], stored_waves.shape[-1]
    depth_count, depth_index = lax.axis_size("depth"), lax.axis_index("depth")
    waves = stored_waves[0].astype(jnp.float32)
    layers = transmission[0].astype(jnp.float32)

    def product(a, b):
        return jnp.stack(conj_times((a[:, 0], a[:, 1]), (b[:, 0], b[:, 1])), 1)

    adjoint = residual
    for turn in range(1, depth_count):
        handed = product(layers, adjoint).astype(jnp.bfloat16)
        got = lax.ppermute(handed, "depth", [(d, d - 1) for d in range(1, depth_count)])
        active = depth_index == depth_count - 1 - turn
        adjoint = lax.cond(active, lambda: back_propagate(got.astype(jnp.float32)), lambda: adjoint)
    gradient = jnp.moveaxis(product(waves, adjoint), 1, 0)
    corners = offsets[slot_position]

    def add_patch(number, region):
        patch = lax.dynamic_index_in_dim(gradient, number, 1, keepdims=True)
        corner = (0, 0, corners[number, 0], corners[number, 1])
        current = lax.dynamic_slice(region, corner, patch.shape)
        return lax.dynamic_update_slice(region, current + patch, corner)

    region = lax.fori_loop(0, slot_count, add_patch, jnp.zeros((2, 1, OBJ, OBJ), jnp.float32))
    strips = lax.psum_scatter(region, "probe", scatter_dimension=2, tiled=True)
    return lax.psum_scatter(strips, "tile", scatter_dimension=3, tiled=True)


def solution(mesh):
    sizes = dict(mesh.shape)

    def per_device(stored_waves, *rest):
        small = (sizes["depth"], sizes["probe"], sizes["tile"], stored_waves.shape[1]) == (2, 4, 2, 1)
        return (two_slices if small else any_slices)(stored_waves, *rest)

    slots = ("groups", "probe", "tile")
    return jax.shard_map(
        per_device,
        mesh=mesh,
        in_specs=(
            P("depth", slots, None, None, None),
            P("depth", slots, None, None, None),
            P(slots, None, None, None),
            P("groups", None),
            P(slots),
        ),
        out_specs=P("groups", "depth", "probe", "tile"),
        check_vma=False,
    )
```

```python
import functools
import math

import jax
import jax.numpy as jnp
import numpy as np
from jax import lax
from jax.experimental import pallas as pl
from jax.experimental.pallas import tpu as pltpu
from jax.sharding import PartitionSpec as P

OBJ = 512
CORNER_ROWS = 16


def propagator(side):
    counter = np.arange(side)
    frequency = (counter + side // 2) % side - side // 2
    chirp = np.exp(0.5j * frequency.astype(np.float64) ** 2 / side)
    ring = np.fft.ifft(chirp)
    ring = 0.5 * (ring + ring[(-counter) % side])
    matrix = ring[(counter[:, None] - counter[None, :]) % side]
    return np.stack([matrix.real, matrix.imag]).astype(np.float32)


def mm(a, b):
    return jnp.dot(a, b, preferred_element_type=jnp.float32)


def split(x):
    high = x.astype(jnp.bfloat16)
    return high, (x - high.astype(jnp.float32)).astype(jnp.bfloat16)


def rolls(side, cy, cx):
    down = lax.broadcasted_iota(jnp.int32, (side, side), 0)
    along = lax.broadcasted_iota(jnp.int32, (side, side), 1)
    rows = (along == ((down - cy) & (side - 1))).astype(jnp.bfloat16)
    cols = (down == ((along - cx) & (side - 1))).astype(jnp.bfloat16)
    return rows, cols


def rolled(parts, rows, cols):
    side = rows.shape[0]
    moved = mm(jnp.concatenate(parts, axis=0), cols).astype(jnp.bfloat16)
    return [mm(rows, moved[n * side : (n + 1) * side]).astype(jnp.bfloat16) for n in range(len(parts))]


def conj_times(a, b):
    return a[0] * b[0] + a[1] * b[1], a[0] * b[1] - a[1] * b[0]


def own_and_other(half):
    parity = lax.rem(lax.axis_index("probe"), 2)
    return (pl.ds(pl.multiple_of(n * half, half), half) for n in (parity, 1 - parity))


def send_kernel(
    token_ref, slot_ref, offsets_hbm, layer_hbm, table_ref, residual_ref,
    own_ref, other_ref, corner_ref,
    offsets_ref, layer_ref, sems,
):
    side = layer_ref.shape[-1]
    half = side // 2
    del token_ref
    offsets_copy = pltpu.make_async_copy(offsets_hbm, offsets_ref, sems.at[0])
    layer_copy = pltpu.make_async_copy(layer_hbm, layer_ref, sems.at[1])
    offsets_copy.start()
    layer_copy.start()
    offsets_copy.wait()
    slot = slot_ref[0]
    cy, cx = offsets_ref[0, slot], offsets_ref[1, slot]
    parity = lax.rem(lax.axis_index("probe"), 2)
    down = (cy - parity * half) & (side - 1)
    line = lax.broadcasted_iota(jnp.int32, corner_ref.shape, 0)
    corner_ref[...] = jnp.where(line == 0, cy.astype(jnp.float32), cx.astype(jnp.float32)).astype(jnp.bfloat16)
    top = lax.axis_index("depth") == 1

    def put(part, x):
        own_ref[part] = x[:half]
        other_ref[part] = x[half:]

    @pl.when(top)
    def _():
        (rhr, rlr), (rhi, rli) = (split(pltpu.roll(table_ref[n], cx, 1)) for n in range(2))
        (lhr, llr), (lhi, lli) = (split(pltpu.roll(table_ref[n], (side - down) & (side - 1), 1)) for n in range(2))
        layer_copy.wait()
        layer = layer_ref[0].astype(jnp.float32), layer_ref[1].astype(jnp.float32)
        handed = conj_times(layer, (residual_ref[0], residual_ref[1]))
        vr, vi = (x.astype(jnp.bfloat16) for x in handed)
        field = jnp.concatenate([vr, vr, vi, vi], axis=1)
        middle = (
            mm(field, jnp.concatenate([rlr, rhr, -rli, -rhi], axis=0)),
            mm(field, jnp.concatenate([rli, rhi, rlr, rhr], axis=0)),
        )
        (mhr, mlr), (mhi, mli) = map(split, middle)
        field = jnp.concatenate([mlr, mhr, mhr, mli, mhi, mhi], axis=0)
        for part, x in enumerate(([lhr, llr, lhr, -lhi, -lli, -lhi], [lhi, lli, lhi, lhr, llr, lhr])):
            put(part, mm(jnp.concatenate(x, axis=1), field).astype(jnp.bfloat16))

    @pl.when(jnp.logical_not(top))
    def _():
        layer_copy.wait()
        rows, cols = rolls(side, down, cx)
        for part, x in enumerate(rolled([residual_ref[n].astype(jnp.bfloat16) for n in range(2)], rows, cols)):
            put(part, x)


def waves_kernel(c0, c1, w0, w1, near_ref, next_ref):
    side = w0.shape[-1]
    half = side // 2
    parity = lax.rem(lax.axis_index("probe"), 2)
    down = lax.broadcasted_iota(jnp.int32, (half, side), 0) + parity * half
    along = lax.broadcasted_iota(jnp.int32, (half, side), 1)
    every = lax.broadcasted_iota(jnp.int32, (side, side), 0)
    across = lax.broadcasted_iota(jnp.int32, (side, side), 1)
    for corner, w, out in ((c0, w0, near_ref), (c1, w1, next_ref)):
        corner = corner[...].astype(jnp.float32)
        cy, cx = corner[0:1].astype(jnp.int32), corner[1:2].astype(jnp.int32)
        rows = (along == ((down - cy) & (side - 1))).astype(jnp.bfloat16)
        cols = (every == ((across - cx) & (side - 1))).astype(jnp.bfloat16)
        moved = mm(rows, jnp.concatenate([w[0], w[1]], axis=1)).astype(jnp.bfloat16)
        moved = mm(jnp.concatenate([moved[:, :side], moved[:, side:]], axis=0), cols).astype(jnp.bfloat16)
        out[0] = moved[:half]
        out[1] = moved[half:]


def sums_kernel(near, c0, c1, a0, a1, w0, w1, here_ref, side_ref):
    half, side = a0.shape[1:]
    place = lax.axis_index("probe")
    strip = (place >= 2) == near
    right = lax.axis_index("tile") == 1
    down = lax.broadcasted_iota(jnp.int32, (half, side), 0) + lax.rem(place, 2) * half
    along = lax.broadcasted_iota(jnp.int32, (half, side), 1)
    zero = jnp.zeros((half, side), jnp.float32)
    here = side_sums = (zero, zero)
    for corner, w, a in ((c0, w0, a0), (c1, w1, a1)):
        corner = corner[...].astype(jnp.float32)
        cy, cx = corner[0:1].astype(jnp.int32), corner[1:2].astype(jnp.int32)
        wave, adjoint = ((x[0].astype(jnp.float32), x[1].astype(jnp.float32)) for x in (w, a))
        inside, own = (down < cy) == strip, (along < cx) == right
        gradient = [jnp.where(inside, x, zero) for x in conj_times(wave, adjoint)]
        here = [total + jnp.where(own, x, zero) for total, x in zip(here, gradient)]
        side_sums = [total + jnp.where(own, zero, x) for total, x in zip(side_sums, gradient)]
    for part in range(2):
        here_ref[part] = here[part]
        side_ref[part] = side_sums[part].astype(jnp.bfloat16)


def token_kernel(out_ref):
    out_ref[...] = jnp.zeros_like(out_ref)


def in_hbm(*arrays):
    return [pltpu.with_memory_space_constraint(x, pltpu.HBM) for x in arrays]


def two_slices(stored_waves, transmission, residual, offsets, slot_position):
    side = stored_waves.shape[-1]
    half = side // 2
    table = jnp.asarray(propagator(side))
    vmem, smem, hbm = (pl.BlockSpec(memory_space=m) for m in (pltpu.VMEM, pltpu.SMEM, pltpu.HBM))
    block, sums = (jax.ShapeDtypeStruct((2, half, side), t) for t in (jnp.bfloat16, jnp.float32))
    params = pltpu.CompilerParams(vmem_limit_bytes=32 * 1024 * 1024)
    by_column = offsets.T
    token = pl.pallas_call(
        token_kernel,
        out_shape=jax.ShapeDtypeStruct((8, 128), jnp.float32),
        out_specs=vmem,
        compiler_params=params,
        cost_estimate=pl.CostEstimate(flops=3 * 10**8, bytes_accessed=0, transcendentals=0),
        name="token",
    )()
    waves, token = lax.optimization_barrier((stored_waves[0, 0], token))
    adj_own, adj_other, corner = pl.pallas_call(
        send_kernel,
        out_shape=(block, block, jax.ShapeDtypeStruct((CORNER_ROWS, side), jnp.bfloat16)),
        in_specs=[vmem, smem, hbm, hbm, vmem, vmem],
        out_specs=(vmem,) * 3,
        scratch_shapes=[
            pltpu.SMEM(by_column.shape, jnp.int32),
            pltpu.VMEM((2, side, side), jnp.bfloat16),
            pltpu.SemaphoreType.DMA((2,)),
        ],
        compiler_params=params,
        name="adjoint",
    )(token, slot_position, *in_hbm(by_column, transmission[0, 0]), table, residual[0])

    probe_count = lax.axis_size("probe")
    swap_tile = [(0, 1), (1, 0)]
    flip = [(2 * z + d, 2 * z + 1 - d) for z in range(probe_count) for d in range(2)]
    flip_z1 = [(2 * z + d, 2 * (z ^ 1) + 1 - d) for z in range(probe_count) for d in range(2)]
    z1 = [(z, z ^ 1) for z in range(probe_count)]
    z2 = [(z, z ^ 2) for z in range(probe_count)]
    a_own = lax.ppermute(adj_own, ("probe", "depth"), flip)
    a_next = lax.ppermute(adj_other, ("probe", "depth"), flip_z1)
    w_next = lax.ppermute(waves, "probe", z1)
    corner_next = lax.ppermute(corner, "probe", z1)
    w_own, w_next = pl.pallas_call(
        waves_kernel,
        out_shape=(block, block),
        in_specs=[vmem] * 4,
        out_specs=(vmem,) * 2,
        compiler_params=params,
        name="rolled_waves",
    )(corner, corner_next, waves, w_next)
    (send, side_send), (keep, side_keep) = (
        pl.pallas_call(
            functools.partial(sums_kernel, near),
            out_shape=(sums, block),
            in_specs=[vmem] * 6,
            out_specs=(vmem,) * 2,
            compiler_params=params,
            name="near_sums" if near else "far_sums",
        )(corner, corner_next, a_own, a_next, w_own, w_next)
        for near in (False, True)
    )
    send = (send + lax.ppermute(side_send, "tile", swap_tile).astype(jnp.float32)).astype(jnp.bfloat16)
    got = lax.ppermute(send, "probe", z2)
    keep = keep + lax.ppermute(side_keep, "tile", swap_tile).astype(jnp.float32)
    return (keep + got.astype(jnp.float32))[:, None]


def times(a, b, spec):
    return jnp.einsum(spec, a, b, precision=lax.Precision.HIGHEST)


def back_propagate(field):
    side = field.shape[-1]
    real, imag = jnp.asarray(propagator(side))
    for spec in ("kn,pnm->pkm", "mk,pnm->pnk"):
        fr, fi = field[:, 0], field[:, 1]
        field = jnp.stack(
            [times(real, fr, spec) - times(imag, fi, spec), times(real, fi, spec) + times(imag, fr, spec)], 1
        )
    return field


def any_slices(stored_waves, transmission, residual, offsets, slot_position):
    slot_count, side = stored_waves.shape[1], stored_waves.shape[-1]
    depth_count, depth_index = lax.axis_size("depth"), lax.axis_index("depth")
    waves = stored_waves[0].astype(jnp.float32)
    layers = transmission[0].astype(jnp.float32)

    def product(a, b):
        return jnp.stack(conj_times((a[:, 0], a[:, 1]), (b[:, 0], b[:, 1])), 1)

    adjoint = residual
    for turn in range(1, depth_count):
        handed = product(layers, adjoint).astype(jnp.bfloat16)
        got = lax.ppermute(handed, "depth", [(d, d - 1) for d in range(1, depth_count)])
        active = depth_index == depth_count - 1 - turn
        adjoint = lax.cond(active, lambda: back_propagate(got.astype(jnp.float32)), lambda: adjoint)
    gradient = jnp.moveaxis(product(waves, adjoint), 1, 0)
    corners = offsets[slot_position]

    def add_patch(number, region):
        patch = lax.dynamic_index_in_dim(gradient, number, 1, keepdims=True)
        corner = (0, 0, corners[number, 0], corners[number, 1])
        current = lax.dynamic_slice(region, corner, patch.shape)
        return lax.dynamic_update_slice(region, current + patch, corner)

    region = lax.fori_loop(0, slot_count, add_patch, jnp.zeros((2, 1, OBJ, OBJ), jnp.float32))
    strips = lax.psum_scatter(region, "probe", scatter_dimension=2, tiled=True)
    return lax.psum_scatter(strips, "tile", scatter_dimension=3, tiled=True)


def solution(mesh):
    sizes = dict(mesh.shape)

    def per_device(stored_waves, *rest):
        small = (sizes["depth"], sizes["probe"], sizes["tile"], stored_waves.shape[1]) == (2, 4, 2, 1)
        return (two_slices if small else any_slices)(stored_waves, *rest)

    slots = ("groups", "probe", "tile")
    return jax.shard_map(
        per_device,
        mesh=mesh,
        in_specs=(
            P("depth", slots, None, None, None),
            P("depth", slots, None, None, None),
            P(slots, None, None, None),
            P("groups", None),
            P(slots),
        ),
        out_specs=P("groups", "depth", "probe", "tile"),
        check_vma=False,
    )
```

```python
import functools
import math

import jax
import jax.numpy as jnp
import numpy as np
from jax import lax
from jax.experimental import pallas as pl
from jax.experimental.pallas import tpu as pltpu
from jax.sharding import PartitionSpec as P

OBJ = 512
CORNER_ROWS = 16


def propagator(side):
    counter = np.arange(side)
    frequency = (counter + side // 2) % side - side // 2
    chirp = np.exp(0.5j * frequency.astype(np.float64) ** 2 / side)
    ring = np.fft.ifft(chirp)
    ring = 0.5 * (ring + ring[(-counter) % side])
    matrix = ring[(counter[:, None] - counter[None, :]) % side]
    return np.stack([matrix.real, matrix.imag]).astype(np.float32)


def mm(a, b):
    return jnp.dot(a, b, preferred_element_type=jnp.float32)


def split(x):
    high = x.astype(jnp.bfloat16)
    return high, (x - high.astype(jnp.float32)).astype(jnp.bfloat16)


def rolls(side, cy, cx):
    down = lax.broadcasted_iota(jnp.int32, (side, side), 0)
    along = lax.broadcasted_iota(jnp.int32, (side, side), 1)
    rows = (along == ((down - cy) & (side - 1))).astype(jnp.bfloat16)
    cols = (down == ((along - cx) & (side - 1))).astype(jnp.bfloat16)
    return rows, cols


def rolled(parts, rows, cols):
    side = rows.shape[0]
    moved = mm(jnp.concatenate(parts, axis=0), cols).astype(jnp.bfloat16)
    return [mm(rows, moved[n * side : (n + 1) * side]).astype(jnp.bfloat16) for n in range(len(parts))]


def conj_times(a, b):
    return a[0] * b[0] + a[1] * b[1], a[0] * b[1] - a[1] * b[0]


def own_and_other(half):
    parity = lax.rem(lax.axis_index("probe"), 2)
    return (pl.ds(pl.multiple_of(n * half, half), half) for n in (parity, 1 - parity))


def send_kernel(
    token_ref, slot_ref, offsets_hbm, layer_hbm, table_ref, residual_ref,
    own_ref, other_ref, corner_ref,
    offsets_ref, layer_ref, sems,
):
    side = layer_ref.shape[-1]
    half = side // 2
    del token_ref
    offsets_copy = pltpu.make_async_copy(offsets_hbm, offsets_ref, sems.at[0])
    layer_copy = pltpu.make_async_copy(layer_hbm, layer_ref, sems.at[1])
    offsets_copy.start()
    layer_copy.start()
    offsets_copy.wait()
    slot = slot_ref[0]
    cy, cx = offsets_ref[0, slot], offsets_ref[1, slot]
    parity = lax.rem(lax.axis_index("probe"), 2)
    down = (cy - parity * half) & (side - 1)
    line = lax.broadcasted_iota(jnp.int32, corner_ref.shape, 0)
    corner_ref[...] = jnp.where(line == 0, cy.astype(jnp.float32), cx.astype(jnp.float32)).astype(jnp.bfloat16)
    top = lax.axis_index("depth") == 1

    def put(part, x):
        own_ref[part] = x[:half]
        other_ref[part] = x[half:]

    @pl.when(top)
    def _():
        (rhr, rlr), (rhi, rli) = (split(pltpu.roll(table_ref[n], cx, 1)) for n in range(2))
        (lhr, llr), (lhi, lli) = (split(pltpu.roll(table_ref[n], (side - down) & (side - 1), 1)) for n in range(2))
        layer_copy.wait()
        layer = layer_ref[0].astype(jnp.float32), layer_ref[1].astype(jnp.float32)
        handed = conj_times(layer, (residual_ref[0], residual_ref[1]))
        vr, vi = (x.astype(jnp.bfloat16) for x in handed)
        field = jnp.concatenate([vr, vr, vi, vi], axis=1)
        middle = (
            mm(field, jnp.concatenate([rlr, rhr, -rli, -rhi], axis=0)),
            mm(field, jnp.concatenate([rli, rhi, rlr, rhr], axis=0)),
        )
        (mhr, mlr), (mhi, mli) = map(split, middle)
        field = jnp.concatenate([mlr, mhr, mhr, mli, mhi, mhi], axis=0)
        for part, x in enumerate(([lhr, llr, lhr, -lhi, -lli, -lhi], [lhi, lli, lhi, lhr, llr, lhr])):
            put(part, mm(jnp.concatenate(x, axis=1), field).astype(jnp.bfloat16))

    @pl.when(jnp.logical_not(top))
    def _():
        layer_copy.wait()
        rows, cols = rolls(side, down, cx)
        for part, x in enumerate(rolled([residual_ref[n].astype(jnp.bfloat16) for n in range(2)], rows, cols)):
            put(part, x)


def waves_kernel(c0, c1, w0, w1, near_ref, next_ref):
    side = w0.shape[-1]
    half = side // 2
    parity = lax.rem(lax.axis_index("probe"), 2)
    down = lax.broadcasted_iota(jnp.int32, (half, side), 0) + parity * half
    along = lax.broadcasted_iota(jnp.int32, (half, side), 1)
    every = lax.broadcasted_iota(jnp.int32, (side, side), 0)
    across = lax.broadcasted_iota(jnp.int32, (side, side), 1)
    for corner, w, out in ((c0, w0, near_ref), (c1, w1, next_ref)):
        corner = corner[...].astype(jnp.float32)
        cy, cx = corner[0:1].astype(jnp.int32), corner[1:2].astype(jnp.int32)
        rows = (along == ((down - cy) & (side - 1))).astype(jnp.bfloat16)
        cols = (every == ((across - cx) & (side - 1))).astype(jnp.bfloat16)
        moved = mm(rows, jnp.concatenate([w[0], w[1]], axis=1)).astype(jnp.bfloat16)
        moved = mm(jnp.concatenate([moved[:, :side], moved[:, side:]], axis=0), cols).astype(jnp.bfloat16)
        out[0] = moved[:half]
        out[1] = moved[half:]


def sums_kernel(near, c0, c1, a0, a1, w0, w1, here_ref, side_ref):
    half, side = a0.shape[1:]
    place = lax.axis_index("probe")
    strip = (place >= 2) == near
    right = lax.axis_index("tile") == 1
    down = lax.broadcasted_iota(jnp.int32, (half, side), 0) + lax.rem(place, 2) * half
    along = lax.broadcasted_iota(jnp.int32, (half, side), 1)
    zero = jnp.zeros((half, side), jnp.float32)
    here = side_sums = (zero, zero)
    for corner, w, a in ((c0, w0, a0), (c1, w1, a1)):
        corner = corner[...].astype(jnp.float32)
        cy, cx = corner[0:1].astype(jnp.int32), corner[1:2].astype(jnp.int32)
        wave, adjoint = ((x[0].astype(jnp.float32), x[1].astype(jnp.float32)) for x in (w, a))
        inside, own = (down < cy) == strip, (along < cx) == right
        gradient = [jnp.where(inside, x, zero) for x in conj_times(wave, adjoint)]
        here = [total + jnp.where(own, x, zero) for total, x in zip(here, gradient)]
        side_sums = [total + jnp.where(own, zero, x) for total, x in zip(side_sums, gradient)]
    for part in range(2):
        here_ref[part] = here[part]
        side_ref[part] = side_sums[part].astype(jnp.bfloat16)


def copy_kernel(in_ref, *refs):
    refs[-1][...] = in_ref[...]


def token_kernel(out_ref):
    out_ref[...] = jnp.zeros_like(out_ref)


def in_hbm(*arrays):
    return [pltpu.with_memory_space_constraint(x, pltpu.HBM) for x in arrays]


def two_slices(stored_waves, transmission, residual, offsets, slot_position):
    side = stored_waves.shape[-1]
    half = side // 2
    table = jnp.asarray(propagator(side))
    vmem, smem, hbm = (pl.BlockSpec(memory_space=m) for m in (pltpu.VMEM, pltpu.SMEM, pltpu.HBM))
    block, sums = (jax.ShapeDtypeStruct((2, half, side), t) for t in (jnp.bfloat16, jnp.float32))
    params = pltpu.CompilerParams(vmem_limit_bytes=32 * 1024 * 1024)
    by_column = offsets.T
    token = pl.pallas_call(
        token_kernel,
        out_shape=jax.ShapeDtypeStruct((8, 128), jnp.float32),
        out_specs=vmem,
        compiler_params=params,
        cost_estimate=pl.CostEstimate(flops=3 * 10**8, bytes_accessed=0, transcendentals=0),
        name="token",
    )()
    waves, token = lax.optimization_barrier((stored_waves[0, 0], token))
    adj_own, adj_other, corner = pl.pallas_call(
        send_kernel,
        out_shape=(block, block, jax.ShapeDtypeStruct((CORNER_ROWS, side), jnp.bfloat16)),
        in_specs=[vmem, smem, hbm, hbm, vmem, vmem],
        out_specs=(vmem,) * 3,
        scratch_shapes=[
            pltpu.SMEM(by_column.shape, jnp.int32),
            pltpu.VMEM((2, side, side), jnp.bfloat16),
            pltpu.SemaphoreType.DMA((2,)),
        ],
        compiler_params=params,
        name="adjoint",
    )(token, slot_position, *in_hbm(by_column, transmission[0, 0]), table, residual[0])

    probe_count = lax.axis_size("probe")
    swap_tile = [(0, 1), (1, 0)]
    flip = [(2 * z + d, 2 * z + 1 - d) for z in range(probe_count) for d in range(2)]
    flip_z1 = [(2 * z + d, 2 * (z ^ 1) + 1 - d) for z in range(probe_count) for d in range(2)]
    z1, z2 = ([(z, z ^ n) for z in range(probe_count)] for n in (1, 2))
    a_own = lax.ppermute(adj_own, ("probe", "depth"), flip)
    a_next = lax.ppermute(adj_other, ("probe", "depth"), flip_z1)
    w_next = lax.ppermute(waves, "probe", z1)
    corner_next = lax.ppermute(corner, "probe", z1)
    w_own, w_next = pl.pallas_call(
        waves_kernel,
        out_shape=(block, block),
        in_specs=[vmem] * 4,
        out_specs=(vmem,) * 2,
        compiler_params=params,
        name="rolled_waves",
    )(corner, corner_next, waves, w_next)
    (send, side_send), (keep, side_keep) = (
        pl.pallas_call(
            functools.partial(sums_kernel, near),
            out_shape=(sums, block),
            in_specs=[vmem] * 6,
            out_specs=(vmem,) * 2,
            compiler_params=params,
            name="near_sums" if near else "far_sums",
        )(corner, corner_next, a_own, a_next, w_own, w_next)
        for near in (False, True)
    )
    send = (send + lax.ppermute(side_send, "tile", swap_tile).astype(jnp.float32)).astype(jnp.bfloat16)

    def after(x, *earlier):
        return pl.pallas_call(
            copy_kernel,
            out_shape=jax.ShapeDtypeStruct(x.shape, x.dtype),
            in_specs=[vmem] * (1 + len(earlier)),
            out_specs=vmem,
            compiler_params=params,
            name="after",
        )(x, *earlier)

    odd = lax.axis_index("probe") % 2 == 1
    even_far, odd_far = (
        [(2 * z + t, 2 * (z ^ 2) + t if z % 2 == turn else 2 * z + 1 - t) for z in range(probe_count) for t in range(2)]
        for turn in range(2)
    )
    once = lax.ppermute(after(corner, send), "tile", swap_tile)
    first = lax.ppermute(after(send, side_keep), ("probe", "tile"), even_far)
    twice = lax.ppermute(after(corner, once), "tile", swap_tile)
    near = lax.ppermute(after(side_keep, first), "tile", swap_tile)
    third = lax.ppermute(after(send, twice), ("probe", "tile"), odd_far)
    far = jnp.where(odd, third, first)
    return (keep + (near.astype(jnp.float32) + far.astype(jnp.float32)))[:, None]


def times(a, b, spec):
    return jnp.einsum(spec, a, b, precision=lax.Precision.HIGHEST)


def back_propagate(field):
    side = field.shape[-1]
    real, imag = jnp.asarray(propagator(side))
    for spec in ("kn,pnm->pkm", "mk,pnm->pnk"):
        fr, fi = field[:, 0], field[:, 1]
        field = jnp.stack(
            [times(real, fr, spec) - times(imag, fi, spec), times(real, fi, spec) + times(imag, fr, spec)], 1
        )
    return field


def any_slices(stored_waves, transmission, residual, offsets, slot_position):
    slot_count, side = stored_waves.shape[1], stored_waves.shape[-1]
    depth_count, depth_index = lax.axis_size("depth"), lax.axis_index("depth")
    waves = stored_waves[0].astype(jnp.float32)
    layers = transmission[0].astype(jnp.float32)

    def product(a, b):
        return jnp.stack(conj_times((a[:, 0], a[:, 1]), (b[:, 0], b[:, 1])), 1)

    adjoint = residual
    for turn in range(1, depth_count):
        handed = product(layers, adjoint).astype(jnp.bfloat16)
        got = lax.ppermute(handed, "depth", [(d, d - 1) for d in range(1, depth_count)])
        active = depth_index == depth_count - 1 - turn
        adjoint = lax.cond(active, lambda: back_propagate(got.astype(jnp.float32)), lambda: adjoint)
    gradient = jnp.moveaxis(product(waves, adjoint), 1, 0)
    corners = offsets[slot_position]

    def add_patch(number, region):
        patch = lax.dynamic_index_in_dim(gradient, number, 1, keepdims=True)
        corner = (0, 0, corners[number, 0], corners[number, 1])
        current = lax.dynamic_slice(region, corner, patch.shape)
        return lax.dynamic_update_slice(region, current + patch, corner)

    region = lax.fori_loop(0, slot_count, add_patch, jnp.zeros((2, 1, OBJ, OBJ), jnp.float32))
    strips = lax.psum_scatter(region, "probe", scatter_dimension=2, tiled=True)
    return lax.psum_scatter(strips, "tile", scatter_dimension=3, tiled=True)


def solution(mesh):
    sizes = dict(mesh.shape)

    def per_device(stored_waves, *rest):
        small = (sizes["depth"], sizes["probe"], sizes["tile"], stored_waves.shape[1]) == (2, 4, 2, 1)
        return (two_slices if small else any_slices)(stored_waves, *rest)

    slots = ("groups", "probe", "tile")
    return jax.shard_map(
        per_device,
        mesh=mesh,
        in_specs=(
            P("depth", slots, None, None, None),
            P("depth", slots, None, None, None),
            P(slots, None, None, None),
            P("groups", None),
            P(slots),
        ),
        out_specs=P("groups", "depth", "probe", "tile"),
        check_vma=False,
    )
```

```python
import functools
import math

import jax
import jax.numpy as jnp
import numpy as np
from jax import lax
from jax.experimental import pallas as pl
from jax.experimental.pallas import tpu as pltpu
from jax.sharding import PartitionSpec as P

OBJ = 512
CORNER_ROWS = 16


def propagator(side):
    counter = np.arange(side)
    frequency = (counter + side // 2) % side - side // 2
    chirp = np.exp(0.5j * frequency.astype(np.float64) ** 2 / side)
    ring = np.fft.ifft(chirp)
    ring = 0.5 * (ring + ring[(-counter) % side])
    matrix = ring[(counter[:, None] - counter[None, :]) % side]
    return np.stack([matrix.real, matrix.imag]).astype(np.float32)


def mm(a, b):
    return jnp.dot(a, b, preferred_element_type=jnp.float32)


def split(x):
    high = x.astype(jnp.bfloat16)
    return high, (x - high.astype(jnp.float32)).astype(jnp.bfloat16)


def rolls(side, cy, cx):
    down = lax.broadcasted_iota(jnp.int32, (side, side), 0)
    along = lax.broadcasted_iota(jnp.int32, (side, side), 1)
    rows = (along == ((down - cy) & (side - 1))).astype(jnp.bfloat16)
    cols = (down == ((along - cx) & (side - 1))).astype(jnp.bfloat16)
    return rows, cols


def rolled(parts, rows, cols):
    side = rows.shape[0]
    moved = mm(jnp.concatenate(parts, axis=0), cols).astype(jnp.bfloat16)
    return [mm(rows, moved[n * side : (n + 1) * side]).astype(jnp.bfloat16) for n in range(len(parts))]


def conj_times(a, b):
    return a[0] * b[0] + a[1] * b[1], a[0] * b[1] - a[1] * b[0]


def own_and_other(half):
    parity = lax.rem(lax.axis_index("probe"), 2)
    return (pl.ds(pl.multiple_of(n * half, half), half) for n in (parity, 1 - parity))


def send_kernel(
    token_ref, slot_ref, offsets_hbm, layer_hbm, table_ref, residual_ref,
    own_ref, other_ref, corner_ref,
    offsets_ref, layer_ref, sems,
):
    side = layer_ref.shape[-1]
    half = side // 2
    del token_ref
    offsets_copy = pltpu.make_async_copy(offsets_hbm, offsets_ref, sems.at[0])
    layer_copy = pltpu.make_async_copy(layer_hbm, layer_ref, sems.at[1])
    offsets_copy.start()
    layer_copy.start()
    offsets_copy.wait()
    slot = slot_ref[0]
    cy, cx = offsets_ref[0, slot], offsets_ref[1, slot]
    parity = lax.rem(lax.axis_index("probe"), 2)
    down = (cy - parity * half) & (side - 1)
    line = lax.broadcasted_iota(jnp.int32, corner_ref.shape, 0)
    corner_ref[...] = jnp.where(line == 0, cy.astype(jnp.float32), cx.astype(jnp.float32)).astype(jnp.bfloat16)
    top = lax.axis_index("depth") == 1

    def put(part, x):
        own_ref[part] = x[:half]
        other_ref[part] = x[half:]

    @pl.when(top)
    def _():
        layer_copy.wait()
        layer = layer_ref[0].astype(jnp.float32), layer_ref[1].astype(jnp.float32)
        handed = conj_times(layer, (residual_ref[0], residual_ref[1]))
        vr, vi = (x.astype(jnp.bfloat16) for x in handed)
        (rhr, rlr), (rhi, rli) = (split(pltpu.roll(table_ref[n], cx, 1)) for n in range(2))
        field = jnp.concatenate([vr, vr, vi, vi], axis=1)
        middle = (
            mm(field, jnp.concatenate([rlr, rhr, -rli, -rhi], axis=0)),
            mm(field, jnp.concatenate([rli, rhi, rlr, rhr], axis=0)),
        )
        (lhr, llr), (lhi, lli) = (split(pltpu.roll(table_ref[n], (side - down) & (side - 1), 1)) for n in range(2))
        (mhr, mlr), (mhi, mli) = map(split, middle)
        field = jnp.concatenate([mlr, mhr, mhr, mli, mhi, mhi], axis=0)
        for part, x in enumerate(([lhr, llr, lhr, -lhi, -lli, -lhi], [lhi, lli, lhi, lhr, llr, lhr])):
            put(part, mm(jnp.concatenate(x, axis=1), field).astype(jnp.bfloat16))

    @pl.when(jnp.logical_not(top))
    def _():
        layer_copy.wait()
        rows, cols = rolls(side, down, cx)
        for part, x in enumerate(rolled([residual_ref[n].astype(jnp.bfloat16) for n in range(2)], rows, cols)):
            put(part, x)


def waves_kernel(c0, c1, w0, w1, near_ref, next_ref):
    side = w0.shape[-1]
    half = side // 2
    parity = lax.rem(lax.axis_index("probe"), 2)
    down = lax.broadcasted_iota(jnp.int32, (half, side), 0) + parity * half
    along = lax.broadcasted_iota(jnp.int32, (half, side), 1)
    every = lax.broadcasted_iota(jnp.int32, (side, side), 0)
    across = lax.broadcasted_iota(jnp.int32, (side, side), 1)
    for corner, w, out in ((c0, w0, near_ref), (c1, w1, next_ref)):
        corner = corner[...].astype(jnp.float32)
        cy, cx = corner[0:1].astype(jnp.int32), corner[1:2].astype(jnp.int32)
        rows = (along == ((down - cy) & (side - 1))).astype(jnp.bfloat16)
        cols = (every == ((across - cx) & (side - 1))).astype(jnp.bfloat16)
        moved = mm(rows, jnp.concatenate([w[0], w[1]], axis=1)).astype(jnp.bfloat16)
        moved = mm(jnp.concatenate([moved[:, :side], moved[:, side:]], axis=0), cols).astype(jnp.bfloat16)
        out[0] = moved[:half]
        out[1] = moved[half:]


def sums_kernel(near, c0, c1, a0, a1, w0, w1, here_ref, side_ref):
    half, side = a0.shape[1:]
    place = lax.axis_index("probe")
    strip = (place >= 2) == near
    right = lax.axis_index("tile") == 1
    down = lax.broadcasted_iota(jnp.int32, (half, side), 0) + lax.rem(place, 2) * half
    along = lax.broadcasted_iota(jnp.int32, (half, side), 1)
    zero = jnp.zeros((half, side), jnp.float32)
    here = side_sums = (zero, zero)
    for corner, w, a in ((c0, w0, a0), (c1, w1, a1)):
        corner = corner[...].astype(jnp.float32)
        cy, cx = corner[0:1].astype(jnp.int32), corner[1:2].astype(jnp.int32)
        wave, adjoint = ((x[0].astype(jnp.float32), x[1].astype(jnp.float32)) for x in (w, a))
        inside, own = (down < cy) == strip, (along < cx) == right
        gradient = [jnp.where(inside, x, zero) for x in conj_times(wave, adjoint)]
        here = [total + jnp.where(own, x, zero) for total, x in zip(here, gradient)]
        side_sums = [total + jnp.where(own, zero, x) for total, x in zip(side_sums, gradient)]
    for part in range(2):
        here_ref[part] = here[part]
        side_ref[part] = side_sums[part].astype(jnp.bfloat16)


def copy_kernel(in_ref, *refs):
    refs[-1][...] = in_ref[...]


def token_kernel(out_ref):
    out_ref[...] = jnp.zeros_like(out_ref)


def in_hbm(*arrays):
    return [pltpu.with_memory_space_constraint(x, pltpu.HBM) for x in arrays]


def two_slices(stored_waves, transmission, residual, offsets, slot_position):
    side = stored_waves.shape[-1]
    half = side // 2
    table = jnp.asarray(propagator(side))
    vmem, smem, hbm = (pl.BlockSpec(memory_space=m) for m in (pltpu.VMEM, pltpu.SMEM, pltpu.HBM))
    block, sums = (jax.ShapeDtypeStruct((2, half, side), t) for t in (jnp.bfloat16, jnp.float32))
    params = pltpu.CompilerParams(vmem_limit_bytes=32 * 1024 * 1024)
    by_column = offsets.T
    token = pl.pallas_call(
        token_kernel,
        out_shape=jax.ShapeDtypeStruct((8, 128), jnp.float32),
        out_specs=vmem,
        compiler_params=params,
        cost_estimate=pl.CostEstimate(flops=3 * 10**8, bytes_accessed=0, transcendentals=0),
        name="token",
    )()
    waves, token = lax.optimization_barrier((stored_waves[0, 0], token))
    adj_own, adj_other, corner = pl.pallas_call(
        send_kernel,
        out_shape=(block, block, jax.ShapeDtypeStruct((CORNER_ROWS, side), jnp.bfloat16)),
        in_specs=[vmem, smem, hbm, hbm, vmem, vmem],
        out_specs=(vmem,) * 3,
        scratch_shapes=[
            pltpu.SMEM(by_column.shape, jnp.int32),
            pltpu.VMEM((2, side, side), jnp.bfloat16),
            pltpu.SemaphoreType.DMA((2,)),
        ],
        compiler_params=params,
        name="adjoint",
    )(token, slot_position, *in_hbm(by_column, transmission[0, 0]), table, residual[0])

    probe_count = lax.axis_size("probe")
    swap_tile = [(0, 1), (1, 0)]
    flip = [(2 * z + d, 2 * z + 1 - d) for z in range(probe_count) for d in range(2)]
    flip_z1 = [(2 * z + d, 2 * (z ^ 1) + 1 - d) for z in range(probe_count) for d in range(2)]
    z1, z2 = ([(z, z ^ n) for z in range(probe_count)] for n in (1, 2))
    a_own = lax.ppermute(adj_own, ("probe", "depth"), flip)
    a_next = lax.ppermute(adj_other, ("probe", "depth"), flip_z1)
    w_next = lax.ppermute(waves, "probe", z1)
    corner_next = lax.ppermute(corner, "probe", z1)
    w_own, w_next = pl.pallas_call(
        waves_kernel,
        out_shape=(block, block),
        in_specs=[vmem] * 4,
        out_specs=(vmem,) * 2,
        compiler_params=params,
        name="rolled_waves",
    )(corner, corner_next, waves, w_next)
    (send, side_send), (keep, side_keep) = (
        pl.pallas_call(
            functools.partial(sums_kernel, near),
            out_shape=(sums, block),
            in_specs=[vmem] * 6,
            out_specs=(vmem,) * 2,
            compiler_params=params,
            name="near_sums" if near else "far_sums",
        )(corner, corner_next, a_own, a_next, w_own, w_next)
        for near in (False, True)
    )
    send = (send + lax.ppermute(side_send, "tile", swap_tile).astype(jnp.float32)).astype(jnp.bfloat16)

    def after(x, *earlier):
        return pl.pallas_call(
            copy_kernel,
            out_shape=jax.ShapeDtypeStruct(x.shape, x.dtype),
            in_specs=[vmem] * (1 + len(earlier)),
            out_specs=vmem,
            compiler_params=params,
            name="after",
        )(x, *earlier)

    odd = lax.axis_index("probe") % 2 == 1
    even_far, odd_far = (
        [(2 * z + t, 2 * (z ^ 2) + t if z % 2 == turn else 2 * z + 1 - t) for z in range(probe_count) for t in range(2)]
        for turn in range(2)
    )
    once = lax.ppermute(after(corner, send), "tile", swap_tile)
    first = lax.ppermute(after(send, side_keep), ("probe", "tile"), even_far)
    twice = lax.ppermute(after(corner, once), "tile", swap_tile)
    near = lax.ppermute(after(side_keep, first), "tile", swap_tile)
    third = lax.ppermute(after(send, twice), ("probe", "tile"), odd_far)
    far = jnp.where(odd, third, first)
    return (keep + (near.astype(jnp.float32) + far.astype(jnp.float32)))[:, None]


def times(a, b, spec):
    return jnp.einsum(spec, a, b, precision=lax.Precision.HIGHEST)


def back_propagate(field):
    side = field.shape[-1]
    real, imag = jnp.asarray(propagator(side))
    for spec in ("kn,pnm->pkm", "mk,pnm->pnk"):
        fr, fi = field[:, 0], field[:, 1]
        field = jnp.stack(
            [times(real, fr, spec) - times(imag, fi, spec), times(real, fi, spec) + times(imag, fr, spec)], 1
        )
    return field


def any_slices(stored_waves, transmission, residual, offsets, slot_position):
    slot_count, side = stored_waves.shape[1], stored_waves.shape[-1]
    depth_count, depth_index = lax.axis_size("depth"), lax.axis_index("depth")
    waves = stored_waves[0].astype(jnp.float32)
    layers = transmission[0].astype(jnp.float32)

    def product(a, b):
        return jnp.stack(conj_times((a[:, 0], a[:, 1]), (b[:, 0], b[:, 1])), 1)

    adjoint = residual
    for turn in range(1, depth_count):
        handed = product(layers, adjoint).astype(jnp.bfloat16)
        got = lax.ppermute(handed, "depth", [(d, d - 1) for d in range(1, depth_count)])
        active = depth_index == depth_count - 1 - turn
        adjoint = lax.cond(active, lambda: back_propagate(got.astype(jnp.float32)), lambda: adjoint)
    gradient = jnp.moveaxis(product(waves, adjoint), 1, 0)
    corners = offsets[slot_position]

    def add_patch(number, region):
        patch = lax.dynamic_index_in_dim(gradient, number, 1, keepdims=True)
        corner = (0, 0, corners[number, 0], corners[number, 1])
        current = lax.dynamic_slice(region, corner, patch.shape)
        return lax.dynamic_update_slice(region, current + patch, corner)

    region = lax.fori_loop(0, slot_count, add_patch, jnp.zeros((2, 1, OBJ, OBJ), jnp.float32))
    strips = lax.psum_scatter(region, "probe", scatter_dimension=2, tiled=True)
    return lax.psum_scatter(strips, "tile", scatter_dimension=3, tiled=True)


def solution(mesh):
    sizes = dict(mesh.shape)

    def per_device(stored_waves, *rest):
        small = (sizes["depth"], sizes["probe"], sizes["tile"], stored_waves.shape[1]) == (2, 4, 2, 1)
        return (two_slices if small else any_slices)(stored_waves, *rest)

    slots = ("groups", "probe", "tile")
    return jax.shard_map(
        per_device,
        mesh=mesh,
        in_specs=(
            P("depth", slots, None, None, None),
            P("depth", slots, None, None, None),
            P(slots, None, None, None),
            P("groups", None),
            P(slots),
        ),
        out_specs=P("groups", "depth", "probe", "tile"),
        check_vma=False,
    )
```

```python
import functools

import jax
import jax.numpy as jnp
import numpy as np
from jax import lax
from jax.experimental import pallas as pl
from jax.experimental.pallas import tpu as pltpu
from jax.sharding import PartitionSpec as P

OBJ = 512
CORNER_ROWS = 16


def propagator(side):
    counter = np.arange(side)
    frequency = (counter + side // 2) % side - side // 2
    chirp = np.exp(0.5j * frequency.astype(np.float64) ** 2 / side)
    ring = np.fft.ifft(chirp)
    ring = 0.5 * (ring + ring[(-counter) % side])
    matrix = ring[(counter[:, None] - counter[None, :]) % side]
    return np.stack([matrix.real, matrix.imag]).astype(np.float32)


def mm(a, b):
    return jnp.dot(a, b, preferred_element_type=jnp.float32)


def split(x):
    high = x.astype(jnp.bfloat16)
    return high, (x - high.astype(jnp.float32)).astype(jnp.bfloat16)


def rolls(side, cy, cx):
    down = lax.broadcasted_iota(jnp.int32, (side, side), 0)
    along = lax.broadcasted_iota(jnp.int32, (side, side), 1)
    rows = (along == ((down - cy) & (side - 1))).astype(jnp.bfloat16)
    cols = (down == ((along - cx) & (side - 1))).astype(jnp.bfloat16)
    return rows, cols


def rolled(parts, rows, cols):
    side = rows.shape[0]
    moved = mm(jnp.concatenate(parts, axis=0), cols).astype(jnp.bfloat16)
    return [mm(rows, moved[n * side : (n + 1) * side]).astype(jnp.bfloat16) for n in range(len(parts))]


def conj_times(a, b):
    return a[0] * b[0] + a[1] * b[1], a[0] * b[1] - a[1] * b[0]


def send_kernel(
    early_ref, slot_ref, offsets_hbm, layer_hbm, table_ref, residual_ref,
    own_ref, other_ref, corner_ref,
    offsets_ref, layer_ref, sems,
):
    side = layer_ref.shape[-1]
    half = side // 2
    del early_ref
    offsets_copy = pltpu.make_async_copy(offsets_hbm, offsets_ref, sems.at[0])
    layer_copy = pltpu.make_async_copy(layer_hbm, layer_ref, sems.at[1])
    offsets_copy.start()
    layer_copy.start()
    offsets_copy.wait()
    slot = slot_ref[0]
    cy, cx = offsets_ref[0, slot], offsets_ref[1, slot]
    parity = lax.rem(lax.axis_index("probe"), 2)
    down = (cy - parity * half) & (side - 1)
    line = lax.broadcasted_iota(jnp.int32, corner_ref.shape, 0)
    corner_ref[...] = jnp.where(line == 0, cy.astype(jnp.float32), cx.astype(jnp.float32)).astype(jnp.bfloat16)
    top = lax.axis_index("depth") == 1

    def put(part, x):
        own_ref[part] = x[:half]
        other_ref[part] = x[half:]

    @pl.when(top)
    def _():
        layer_copy.wait()
        layer = layer_ref[0].astype(jnp.float32), layer_ref[1].astype(jnp.float32)
        handed = conj_times(layer, (residual_ref[0], residual_ref[1]))
        vr, vi = (x.astype(jnp.bfloat16) for x in handed)
        (rhr, rlr), (rhi, rli) = (split(pltpu.roll(table_ref[n], cx, 1)) for n in range(2))
        field = jnp.concatenate([vr, vr, vi, vi], axis=1)
        middle = (
            mm(field, jnp.concatenate([rlr, rhr, -rli, -rhi], axis=0)),
            mm(field, jnp.concatenate([rli, rhi, rlr, rhr], axis=0)),
        )
        (lhr, llr), (lhi, lli) = (split(pltpu.roll(table_ref[n], (side - down) & (side - 1), 1)) for n in range(2))
        (mhr, mlr), (mhi, mli) = map(split, middle)
        field = jnp.concatenate([mlr, mhr, mhr, mli, mhi, mhi], axis=0)
        for part, x in enumerate(([lhr, llr, lhr, -lhi, -lli, -lhi], [lhi, lli, lhi, lhr, llr, lhr])):
            put(part, mm(jnp.concatenate(x, axis=1), field).astype(jnp.bfloat16))

    @pl.when(jnp.logical_not(top))
    def _():
        layer_copy.wait()
        rows, cols = rolls(side, down, cx)
        for part, x in enumerate(rolled([residual_ref[n].astype(jnp.bfloat16) for n in range(2)], rows, cols)):
            put(part, x)


def waves_kernel(c0, c1, w0, w1, near_ref, next_ref):
    side = w0.shape[-1]
    half = side // 2
    parity = lax.rem(lax.axis_index("probe"), 2)
    down = lax.broadcasted_iota(jnp.int32, (half, side), 0) + parity * half
    along = lax.broadcasted_iota(jnp.int32, (half, side), 1)
    every = lax.broadcasted_iota(jnp.int32, (side, side), 0)
    across = lax.broadcasted_iota(jnp.int32, (side, side), 1)
    for corner, w, out in ((c0, w0, near_ref), (c1, w1, next_ref)):
        corner = corner[...].astype(jnp.float32)
        cy, cx = corner[0:1].astype(jnp.int32), corner[1:2].astype(jnp.int32)
        rows = (along == ((down - cy) & (side - 1))).astype(jnp.bfloat16)
        cols = (every == ((across - cx) & (side - 1))).astype(jnp.bfloat16)
        moved = mm(rows, jnp.concatenate([w[0], w[1]], axis=1)).astype(jnp.bfloat16)
        moved = mm(jnp.concatenate([moved[:, :side], moved[:, side:]], axis=0), cols).astype(jnp.bfloat16)
        out[0] = moved[:half]
        out[1] = moved[half:]


def sums_kernel(near, c0, c1, a0, a1, w0, w1, here_ref, side_ref):
    half, side = a0.shape[1:]
    place = lax.axis_index("probe")
    strip = (place >= 2) == near
    right = lax.axis_index("tile") == 1
    down = lax.broadcasted_iota(jnp.int32, (half, side), 0) + lax.rem(place, 2) * half
    along = lax.broadcasted_iota(jnp.int32, (half, side), 1)
    zero = jnp.zeros((half, side), jnp.float32)
    here = side_sums = (zero, zero)
    for corner, w, a in ((c0, w0, a0), (c1, w1, a1)):
        corner = corner[...].astype(jnp.float32)
        cy, cx = corner[0:1].astype(jnp.int32), corner[1:2].astype(jnp.int32)
        wave, adjoint = ((x[0].astype(jnp.float32), x[1].astype(jnp.float32)) for x in (w, a))
        inside, own = (down < cy) == strip, (along < cx) == right
        gradient = [jnp.where(inside, x, zero) for x in conj_times(wave, adjoint)]
        here = [total + jnp.where(own, x, zero) for total, x in zip(here, gradient)]
        side_sums = [total + jnp.where(own, zero, x) for total, x in zip(side_sums, gradient)]
    for part in range(2):
        here_ref[part] = here[part]
        side_ref[part] = side_sums[part].astype(jnp.bfloat16)


def copy_kernel(in_ref, *refs):
    refs[-1][...] = in_ref[...]


def early_kernel(out_ref):
    out_ref[...] = jnp.zeros_like(out_ref)


def in_hbm(*arrays):
    return [pltpu.with_memory_space_constraint(x, pltpu.HBM) for x in arrays]


def two_slices(stored_waves, transmission, residual, offsets, slot_position):
    side = stored_waves.shape[-1]
    half = side // 2
    table = jnp.asarray(propagator(side))
    vmem, smem, hbm = (pl.BlockSpec(memory_space=m) for m in (pltpu.VMEM, pltpu.SMEM, pltpu.HBM))
    block, sums = (jax.ShapeDtypeStruct((2, half, side), t) for t in (jnp.bfloat16, jnp.float32))
    params = pltpu.CompilerParams(vmem_limit_bytes=32 * 1024 * 1024)
    by_column = offsets.T
    early = pl.pallas_call(
        early_kernel,
        out_shape=jax.ShapeDtypeStruct((8, 128), jnp.float32),
        out_specs=vmem,
        compiler_params=params,
        cost_estimate=pl.CostEstimate(flops=3 * 10**8, bytes_accessed=0, transcendentals=0),
        name="early",
    )()
    waves, early = lax.optimization_barrier((stored_waves[0, 0], early))
    adj_own, adj_other, corner = pl.pallas_call(
        send_kernel,
        out_shape=(block, block, jax.ShapeDtypeStruct((CORNER_ROWS, side), jnp.bfloat16)),
        in_specs=[vmem, smem, hbm, hbm, vmem, vmem],
        out_specs=(vmem,) * 3,
        scratch_shapes=[
            pltpu.SMEM(by_column.shape, jnp.int32),
            pltpu.VMEM((2, side, side), jnp.bfloat16),
            pltpu.SemaphoreType.DMA((2,)),
        ],
        compiler_params=params,
        name="adjoint",
    )(early, slot_position, *in_hbm(by_column, transmission[0, 0]), table, residual[0])

    probe_count = lax.axis_size("probe")
    swap_tile = [(0, 1), (1, 0)]
    flip = [(2 * z + d, 2 * z + 1 - d) for z in range(probe_count) for d in range(2)]
    flip_z1 = [(2 * z + d, 2 * (z ^ 1) + 1 - d) for z in range(probe_count) for d in range(2)]
    z1, z2 = ([(z, z ^ n) for z in range(probe_count)] for n in (1, 2))
    a_own = lax.ppermute(adj_own, ("probe", "depth"), flip)
    a_next = lax.ppermute(adj_other, ("probe", "depth"), flip_z1)
    w_next = lax.ppermute(waves, "probe", z1)
    corner_next = lax.ppermute(corner, "probe", z1)
    w_own, w_next = pl.pallas_call(
        waves_kernel,
        out_shape=(block, block),
        in_specs=[vmem] * 4,
        out_specs=(vmem,) * 2,
        compiler_params=params,
        name="rolled_waves",
    )(corner, corner_next, waves, w_next)
    (send, side_send), (keep, side_keep) = (
        pl.pallas_call(
            functools.partial(sums_kernel, near),
            out_shape=(sums, block),
            in_specs=[vmem] * 6,
            out_specs=(vmem,) * 2,
            compiler_params=params,
            name="near_sums" if near else "far_sums",
        )(corner, corner_next, a_own, a_next, w_own, w_next)
        for near in (False, True)
    )
    send = (send + lax.ppermute(side_send, "tile", swap_tile).astype(jnp.float32)).astype(jnp.bfloat16)

    def after(x, *earlier):
        return pl.pallas_call(
            copy_kernel,
            out_shape=jax.ShapeDtypeStruct(x.shape, x.dtype),
            in_specs=[vmem] * (1 + len(earlier)),
            out_specs=vmem,
            compiler_params=params,
            name="after",
        )(x, *earlier)

    odd = lax.axis_index("probe") % 2 == 1
    even_far, odd_far = (
        [(2 * z + t, 2 * (z ^ 2) + t if z % 2 == turn else 2 * z + 1 - t) for z in range(probe_count) for t in range(2)]
        for turn in range(2)
    )
    once = lax.ppermute(after(corner, send), "tile", swap_tile)
    first = lax.ppermute(after(send, side_keep), ("probe", "tile"), even_far)
    twice = lax.ppermute(after(corner, once), "tile", swap_tile)
    near = lax.ppermute(after(side_keep, first), "tile", swap_tile)
    third = lax.ppermute(after(send, twice), ("probe", "tile"), odd_far)
    far = jnp.where(odd, third, first)
    return (keep + (near.astype(jnp.float32) + far.astype(jnp.float32)))[:, None]


def times(a, b, spec):
    return jnp.einsum(spec, a, b, precision=lax.Precision.HIGHEST)


def back_propagate(field):
    side = field.shape[-1]
    real, imag = jnp.asarray(propagator(side))
    for spec in ("kn,pnm->pkm", "mk,pnm->pnk"):
        fr, fi = field[:, 0], field[:, 1]
        field = jnp.stack(
            [times(real, fr, spec) - times(imag, fi, spec), times(real, fi, spec) + times(imag, fr, spec)], 1
        )
    return field


def any_slices(stored_waves, transmission, residual, offsets, slot_position):
    slot_count, side = stored_waves.shape[1], stored_waves.shape[-1]
    depth_count, depth_index = lax.axis_size("depth"), lax.axis_index("depth")
    waves = stored_waves[0].astype(jnp.float32)
    layers = transmission[0].astype(jnp.float32)

    def product(a, b):
        return jnp.stack(conj_times((a[:, 0], a[:, 1]), (b[:, 0], b[:, 1])), 1)

    adjoint = residual
    for turn in range(1, depth_count):
        handed = product(layers, adjoint).astype(jnp.bfloat16)
        got = lax.ppermute(handed, "depth", [(d, d - 1) for d in range(1, depth_count)])
        active = depth_index == depth_count - 1 - turn
        adjoint = lax.cond(active, lambda: back_propagate(got.astype(jnp.float32)), lambda: adjoint)
    gradient = jnp.moveaxis(product(waves, adjoint), 1, 0)
    corners = offsets[slot_position]

    def add_patch(number, region):
        patch = lax.dynamic_index_in_dim(gradient, number, 1, keepdims=True)
        corner = (0, 0, corners[number, 0], corners[number, 1])
        current = lax.dynamic_slice(region, corner, patch.shape)
        return lax.dynamic_update_slice(region, current + patch, corner)

    region = lax.fori_loop(0, slot_count, add_patch, jnp.zeros((2, 1, OBJ, OBJ), jnp.float32))
    strips = lax.psum_scatter(region, "probe", scatter_dimension=2, tiled=True)
    return lax.psum_scatter(strips, "tile", scatter_dimension=3, tiled=True)


def solution(mesh):
    sizes = dict(mesh.shape)

    def per_device(stored_waves, *rest):
        small = (sizes["depth"], sizes["probe"], sizes["tile"], stored_waves.shape[1]) == (2, 4, 2, 1)
        small = small and 2 * stored_waves.shape[-1] == OBJ
        return (two_slices if small else any_slices)(stored_waves, *rest)

    slots = ("groups", "probe", "tile")
    return jax.shard_map(
        per_device,
        mesh=mesh,
        in_specs=(
            P("depth", slots, None, None, None),
            P("depth", slots, None, None, None),
            P(slots, None, None, None),
            P("groups", None),
            P(slots),
        ),
        out_specs=P("groups", "depth", "probe", "tile"),
        check_vma=False,
    )
```

```python
import functools

import jax
import jax.numpy as jnp
import numpy as np
from jax import lax
from jax.experimental import pallas as pl
from jax.experimental.pallas import tpu as pltpu
from jax.sharding import PartitionSpec as P

OBJ = 512
CORNER_ROWS = 16


def propagator(side):
    counter = np.arange(side)
    frequency = (counter + side // 2) % side - side // 2
    chirp = np.exp(0.5j * frequency.astype(np.float64) ** 2 / side)
    ring = np.fft.ifft(chirp)
    ring = 0.5 * (ring + ring[(-counter) % side])
    matrix = ring[(counter[:, None] - counter[None, :]) % side]
    return np.stack([matrix.real, matrix.imag]).astype(np.float32)


def mm(a, b):
    return jnp.dot(a, b, preferred_element_type=jnp.float32)


def split(x):
    high = x.astype(jnp.bfloat16)
    return high, (x - high.astype(jnp.float32)).astype(jnp.bfloat16)


def rolls(side, cy, cx):
    down = lax.broadcasted_iota(jnp.int32, (side, side), 0)
    along = lax.broadcasted_iota(jnp.int32, (side, side), 1)
    rows = (along == ((down - cy) & (side - 1))).astype(jnp.bfloat16)
    cols = (down == ((along - cx) & (side - 1))).astype(jnp.bfloat16)
    return rows, cols


def rolled(parts, rows, cols):
    side = rows.shape[0]
    moved = mm(jnp.concatenate(parts, axis=0), cols).astype(jnp.bfloat16)
    return [mm(rows, moved[n * side : (n + 1) * side]).astype(jnp.bfloat16) for n in range(len(parts))]


def conj_times(a, b):
    return a[0] * b[0] + a[1] * b[1], a[0] * b[1] - a[1] * b[0]


def send_kernel(
    early_ref, slot_ref, offsets_hbm, layer_hbm, table_ref, residual_ref,
    own_ref, other_ref, corner_ref,
    offsets_ref, layer_ref, sems,
):
    side = layer_ref.shape[-1]
    half = side // 2
    del early_ref
    offsets_copy = pltpu.make_async_copy(offsets_hbm, offsets_ref, sems.at[0])
    layer_copy = pltpu.make_async_copy(layer_hbm, layer_ref, sems.at[1])
    offsets_copy.start()
    layer_copy.start()
    offsets_copy.wait()
    slot = slot_ref[0]
    cy, cx = offsets_ref[0, slot], offsets_ref[1, slot]
    parity = lax.rem(lax.axis_index("probe"), 2)
    down = (cy - parity * half) & (side - 1)
    line = lax.broadcasted_iota(jnp.int32, corner_ref.shape, 0)
    corner_ref[...] = jnp.where(line == 0, cy.astype(jnp.float32), cx.astype(jnp.float32)).astype(jnp.bfloat16)
    top = lax.axis_index("depth") == 1

    def put(part, x):
        own_ref[part] = x[:half]
        other_ref[part] = x[half:]

    @pl.when(top)
    def _():
        layer_copy.wait()
        layer = layer_ref[0].astype(jnp.float32), layer_ref[1].astype(jnp.float32)
        handed = conj_times(layer, (residual_ref[0], residual_ref[1]))
        vr, vi = (x.astype(jnp.bfloat16) for x in handed)
        (rhr, rlr), (rhi, rli) = (split(pltpu.roll(table_ref[n], cx, 1)) for n in range(2))
        field = jnp.concatenate([vr, vr, vi, vi], axis=1)
        middle = (
            mm(field, jnp.concatenate([rlr, rhr, -rli, -rhi], axis=0)),
            mm(field, jnp.concatenate([rli, rhi, rlr, rhr], axis=0)),
        )
        (lhr, llr), (lhi, lli) = (split(pltpu.roll(table_ref[n], (side - down) & (side - 1), 1)) for n in range(2))
        (mhr, mlr), (mhi, mli) = map(split, middle)
        field = jnp.concatenate([mlr, mhr, mhr, mli, mhi, mhi], axis=0)
        for part, x in enumerate(([lhr, llr, lhr, -lhi, -lli, -lhi], [lhi, lli, lhi, lhr, llr, lhr])):
            put(part, mm(jnp.concatenate(x, axis=1), field).astype(jnp.bfloat16))

    @pl.when(jnp.logical_not(top))
    def _():
        layer_copy.wait()
        rows, cols = rolls(side, down, cx)
        for part, x in enumerate(rolled([residual_ref[n].astype(jnp.bfloat16) for n in range(2)], rows, cols)):
            put(part, x)


def waves_kernel(c0, c1, w0, w1, near_ref, next_ref):
    side = w0.shape[-1]
    half = side // 2
    parity = lax.rem(lax.axis_index("probe"), 2)
    down = lax.broadcasted_iota(jnp.int32, (half, side), 0) + parity * half
    along = lax.broadcasted_iota(jnp.int32, (half, side), 1)
    every = lax.broadcasted_iota(jnp.int32, (side, side), 0)
    across = lax.broadcasted_iota(jnp.int32, (side, side), 1)
    for corner, w, out in ((c0, w0, near_ref), (c1, w1, next_ref)):
        corner = corner[...].astype(jnp.float32)
        cy, cx = corner[0:1].astype(jnp.int32), corner[1:2].astype(jnp.int32)
        rows = (along == ((down - cy) & (side - 1))).astype(jnp.bfloat16)
        cols = (every == ((across - cx) & (side - 1))).astype(jnp.bfloat16)
        moved = mm(rows, jnp.concatenate([w[0], w[1]], axis=1)).astype(jnp.bfloat16)
        moved = mm(jnp.concatenate([moved[:, :side], moved[:, side:]], axis=0), cols).astype(jnp.bfloat16)
        out[0] = moved[:half]
        out[1] = moved[half:]


def sums_kernel(near, wanted, c0, c1, a0, a1, w0, w1, *refs):
    half, side = a0.shape[1:]
    place = lax.axis_index("probe")
    strip = (place >= 2) == near
    right = lax.axis_index("tile") == 1
    down = lax.broadcasted_iota(jnp.int32, (half, side), 0) + lax.rem(place, 2) * half
    along = lax.broadcasted_iota(jnp.int32, (half, side), 1)
    zero = jnp.zeros((half, side), jnp.float32)
    here = side_sums = (zero, zero)
    for corner, w, a in ((c0, w0, a0), (c1, w1, a1)):
        corner = corner[...].astype(jnp.float32)
        cy, cx = corner[0:1].astype(jnp.int32), corner[1:2].astype(jnp.int32)
        wave, adjoint = ((x[0].astype(jnp.float32), x[1].astype(jnp.float32)) for x in (w, a))
        inside, own = (down < cy) == strip, (along < cx) == right
        gradient = [jnp.where(inside, x, zero) for x in conj_times(wave, adjoint)]
        here = [total + jnp.where(own, x, zero) for total, x in zip(here, gradient)]
        side_sums = [total + jnp.where(own, zero, x) for total, x in zip(side_sums, gradient)]
    for ref, result in zip(refs, (here, side_sums)[wanted]):
        for part in range(2):
            ref[part] = result[part].astype(ref.dtype)


def copy_kernel(in_ref, *refs):
    refs[-1][...] = in_ref[...]


def early_kernel(out_ref):
    out_ref[...] = jnp.zeros_like(out_ref)


def in_hbm(*arrays):
    return [pltpu.with_memory_space_constraint(x, pltpu.HBM) for x in arrays]


def two_slices(stored_waves, transmission, residual, offsets, slot_position):
    side = stored_waves.shape[-1]
    half = side // 2
    table = jnp.asarray(propagator(side))
    vmem, smem, hbm = (pl.BlockSpec(memory_space=m) for m in (pltpu.VMEM, pltpu.SMEM, pltpu.HBM))
    block, sums = (jax.ShapeDtypeStruct((2, half, side), t) for t in (jnp.bfloat16, jnp.float32))
    params = pltpu.CompilerParams(vmem_limit_bytes=32 * 1024 * 1024)
    by_column = offsets.T
    early = pl.pallas_call(
        early_kernel,
        out_shape=jax.ShapeDtypeStruct((8, 128), jnp.float32),
        out_specs=vmem,
        compiler_params=params,
        cost_estimate=pl.CostEstimate(flops=3 * 10**8, bytes_accessed=0, transcendentals=0),
        name="early",
    )()
    waves, early = lax.optimization_barrier((stored_waves[0, 0], early))
    adj_own, adj_other, corner = pl.pallas_call(
        send_kernel,
        out_shape=(block, block, jax.ShapeDtypeStruct((CORNER_ROWS, side), jnp.bfloat16)),
        in_specs=[vmem, smem, hbm, hbm, vmem, vmem],
        out_specs=(vmem,) * 3,
        scratch_shapes=[
            pltpu.SMEM(by_column.shape, jnp.int32),
            pltpu.VMEM((2, side, side), jnp.bfloat16),
            pltpu.SemaphoreType.DMA((2,)),
        ],
        compiler_params=params,
        name="adjoint",
    )(early, slot_position, *in_hbm(by_column, transmission[0, 0]), table, residual[0])

    probe_count = lax.axis_size("probe")
    swap_tile = [(0, 1), (1, 0)]
    flip = [(2 * z + d, 2 * z + 1 - d) for z in range(probe_count) for d in range(2)]
    flip_z1 = [(2 * z + d, 2 * (z ^ 1) + 1 - d) for z in range(probe_count) for d in range(2)]
    z1, z2 = ([(z, z ^ n) for z in range(probe_count)] for n in (1, 2))
    a_own = lax.ppermute(adj_own, ("probe", "depth"), flip)
    a_next = lax.ppermute(adj_other, ("probe", "depth"), flip_z1)
    w_next = lax.ppermute(waves, "probe", z1)
    corner_next = lax.ppermute(corner, "probe", z1)
    w_own, w_next = pl.pallas_call(
        waves_kernel,
        out_shape=(block, block),
        in_specs=[vmem] * 4,
        out_specs=(vmem,) * 2,
        compiler_params=params,
        name="rolled_waves",
    )(corner, corner_next, waves, w_next)
    def masked_sums(near, wanted, *shapes):
        return pl.pallas_call(
            functools.partial(sums_kernel, near, wanted),
            out_shape=shapes,
            in_specs=[vmem] * 6,
            out_specs=(vmem,) * len(shapes),
            compiler_params=params,
            name="near_sums" if near else "far_sums",
        )(corner, corner_next, a_own, a_next, w_own, w_next)

    (side_send,), (send,) = masked_sums(False, slice(1, 2), block), masked_sums(False, slice(0, 1), sums)
    keep, side_keep = masked_sums(True, slice(0, 2), sums, block)
    send = (send + lax.ppermute(side_send, "tile", swap_tile).astype(jnp.float32)).astype(jnp.bfloat16)

    def after(x, *earlier):
        return pl.pallas_call(
            copy_kernel,
            out_shape=jax.ShapeDtypeStruct(x.shape, x.dtype),
            in_specs=[vmem] * (1 + len(earlier)),
            out_specs=vmem,
            compiler_params=params,
            name="after",
        )(x, *earlier)

    odd = lax.axis_index("probe") % 2 == 1
    even_far, odd_far = (
        [(2 * z + t, 2 * (z ^ 2) + t if z % 2 == turn else 2 * z + 1 - t) for z in range(probe_count) for t in range(2)]
        for turn in range(2)
    )
    once = lax.ppermute(after(corner, send), "tile", swap_tile)
    first = lax.ppermute(after(send, side_keep), ("probe", "tile"), even_far)
    twice = lax.ppermute(after(corner, once), "tile", swap_tile)
    near = lax.ppermute(after(side_keep, first), "tile", swap_tile)
    third = lax.ppermute(after(send, twice), ("probe", "tile"), odd_far)
    far = jnp.where(odd, third, first)
    return (keep + (near.astype(jnp.float32) + far.astype(jnp.float32)))[:, None]


def times(a, b, spec):
    return jnp.einsum(spec, a, b, precision=lax.Precision.HIGHEST)


def back_propagate(field):
    side = field.shape[-1]
    real, imag = jnp.asarray(propagator(side))
    for spec in ("kn,pnm->pkm", "mk,pnm->pnk"):
        fr, fi = field[:, 0], field[:, 1]
        field = jnp.stack(
            [times(real, fr, spec) - times(imag, fi, spec), times(real, fi, spec) + times(imag, fr, spec)], 1
        )
    return field


def any_slices(stored_waves, transmission, residual, offsets, slot_position):
    slot_count, side = stored_waves.shape[1], stored_waves.shape[-1]
    depth_count, depth_index = lax.axis_size("depth"), lax.axis_index("depth")
    waves = stored_waves[0].astype(jnp.float32)
    layers = transmission[0].astype(jnp.float32)

    def product(a, b):
        return jnp.stack(conj_times((a[:, 0], a[:, 1]), (b[:, 0], b[:, 1])), 1)

    adjoint = residual
    for turn in range(1, depth_count):
        handed = product(layers, adjoint).astype(jnp.bfloat16)
        got = lax.ppermute(handed, "depth", [(d, d - 1) for d in range(1, depth_count)])
        active = depth_index == depth_count - 1 - turn
        adjoint = lax.cond(active, lambda: back_propagate(got.astype(jnp.float32)), lambda: adjoint)
    gradient = jnp.moveaxis(product(waves, adjoint), 1, 0)
    corners = offsets[slot_position]

    def add_patch(number, region):
        patch = lax.dynamic_index_in_dim(gradient, number, 1, keepdims=True)
        corner = (0, 0, corners[number, 0], corners[number, 1])
        current = lax.dynamic_slice(region, corner, patch.shape)
        return lax.dynamic_update_slice(region, current + patch, corner)

    region = lax.fori_loop(0, slot_count, add_patch, jnp.zeros((2, 1, OBJ, OBJ), jnp.float32))
    strips = lax.psum_scatter(region, "probe", scatter_dimension=2, tiled=True)
    return lax.psum_scatter(strips, "tile", scatter_dimension=3, tiled=True)


def solution(mesh):
    sizes = dict(mesh.shape)

    def per_device(stored_waves, *rest):
        small = (sizes["depth"], sizes["probe"], sizes["tile"], stored_waves.shape[1]) == (2, 4, 2, 1)
        small = small and 2 * stored_waves.shape[-1] == OBJ
        return (two_slices if small else any_slices)(stored_waves, *rest)

    slots = ("groups", "probe", "tile")
    return jax.shard_map(
        per_device,
        mesh=mesh,
        in_specs=(
            P("depth", slots, None, None, None),
            P("depth", slots, None, None, None),
            P(slots, None, None, None),
            P("groups", None),
            P(slots),
        ),
        out_specs=P("groups", "depth", "probe", "tile"),
        check_vma=False,
    )
```

```python
import functools

import jax
import jax.numpy as jnp
import numpy as np
from jax import lax
from jax.experimental import pallas as pl
from jax.experimental.pallas import tpu as pltpu
from jax.sharding import PartitionSpec as P

OBJ = 512
CORNER_ROWS = 16


def propagator(side):
    counter = np.arange(side)
    frequency = (counter + side // 2) % side - side // 2
    chirp = np.exp(0.5j * frequency.astype(np.float64) ** 2 / side)
    ring = np.fft.ifft(chirp)
    ring = 0.5 * (ring + ring[(-counter) % side])
    matrix = ring[(counter[:, None] - counter[None, :]) % side]
    return np.stack([matrix.real, matrix.imag]).astype(np.float32)


def mm(a, b):
    return jnp.dot(a, b, preferred_element_type=jnp.float32)


def split(x):
    high = x.astype(jnp.bfloat16)
    return high, (x - high.astype(jnp.float32)).astype(jnp.bfloat16)


def rolls(side, cy, cx):
    down = lax.broadcasted_iota(jnp.int32, (side, side), 0)
    along = lax.broadcasted_iota(jnp.int32, (side, side), 1)
    rows = (along == ((down - cy) & (side - 1))).astype(jnp.bfloat16)
    cols = (down == ((along - cx) & (side - 1))).astype(jnp.bfloat16)
    return rows, cols


def rolled(parts, rows, cols):
    side = rows.shape[0]
    moved = mm(jnp.concatenate(parts, axis=0), cols).astype(jnp.bfloat16)
    return [mm(rows, moved[n * side : (n + 1) * side]).astype(jnp.bfloat16) for n in range(len(parts))]


def conj_times(a, b):
    return a[0] * b[0] + a[1] * b[1], a[0] * b[1] - a[1] * b[0]


def send_kernel(
    early_ref, slot_ref, offsets_hbm, layer_hbm, table_ref, residual_ref,
    own_ref, other_ref, corner_ref,
    offsets_ref, layer_ref, sems,
):
    side = layer_ref.shape[-1]
    half = side // 2
    del early_ref
    offsets_copy = pltpu.make_async_copy(offsets_hbm, offsets_ref, sems.at[0])
    layer_copy = pltpu.make_async_copy(layer_hbm, layer_ref, sems.at[1])
    offsets_copy.start()
    layer_copy.start()
    offsets_copy.wait()
    slot = slot_ref[0]
    cy, cx = offsets_ref[0, slot], offsets_ref[1, slot]
    parity = lax.rem(lax.axis_index("probe"), 2)
    down = (cy - parity * half) & (side - 1)
    line = lax.broadcasted_iota(jnp.int32, corner_ref.shape, 0)
    corner_ref[...] = jnp.where(line == 0, cy.astype(jnp.float32), cx.astype(jnp.float32)).astype(jnp.bfloat16)
    top = lax.axis_index("depth") == 1

    def put(part, x):
        own_ref[part] = x[:half]
        other_ref[part] = x[half:]

    @pl.when(top)
    def _():
        layer_copy.wait()
        layer = layer_ref[0].astype(jnp.float32), layer_ref[1].astype(jnp.float32)
        handed = conj_times(layer, (residual_ref[0], residual_ref[1]))
        vr, vi = (x.astype(jnp.bfloat16) for x in handed)
        (rhr, rlr), (rhi, rli) = (split(pltpu.roll(table_ref[n], cx, 1)) for n in range(2))
        field = jnp.concatenate([vr, vr, vi, vi], axis=1)
        middle = (
            mm(field, jnp.concatenate([rlr, rhr, -rli, -rhi], axis=0)),
            mm(field, jnp.concatenate([rli, rhi, rlr, rhr], axis=0)),
        )
        (lhr, llr), (lhi, lli) = (split(pltpu.roll(table_ref[n], (side - down) & (side - 1), 1)) for n in range(2))
        (mhr, mlr), (mhi, mli) = map(split, middle)
        field = jnp.concatenate([mlr, mhr, mhr, mli, mhi, mhi], axis=0)
        for part, x in enumerate(([lhr, llr, lhr, -lhi, -lli, -lhi], [lhi, lli, lhi, lhr, llr, lhr])):
            put(part, mm(jnp.concatenate(x, axis=1), field).astype(jnp.bfloat16))

    @pl.when(jnp.logical_not(top))
    def _():
        layer_copy.wait()
        rows, cols = rolls(side, down, cx)
        for part, x in enumerate(rolled([residual_ref[n].astype(jnp.bfloat16) for n in range(2)], rows, cols)):
            put(part, x)


def waves_kernel(c0, c1, w0, w1, near_ref, next_ref):
    side = w0.shape[-1]
    half = side // 2
    parity = lax.rem(lax.axis_index("probe"), 2)
    down = lax.broadcasted_iota(jnp.int32, (half, side), 0) + parity * half
    along = lax.broadcasted_iota(jnp.int32, (half, side), 1)
    every = lax.broadcasted_iota(jnp.int32, (side, side), 0)
    across = lax.broadcasted_iota(jnp.int32, (side, side), 1)
    for corner, w, out in ((c0, w0, near_ref), (c1, w1, next_ref)):
        corner = corner[...].astype(jnp.float32)
        cy, cx = corner[0:1].astype(jnp.int32), corner[1:2].astype(jnp.int32)
        rows = (along == ((down - cy) & (side - 1))).astype(jnp.bfloat16)
        cols = (every == ((across - cx) & (side - 1))).astype(jnp.bfloat16)
        moved = mm(rows, jnp.concatenate([w[0], w[1]], axis=1)).astype(jnp.bfloat16)
        moved = mm(jnp.concatenate([moved[:, :side], moved[:, side:]], axis=0), cols)
        out[0] = moved[:half]
        out[1] = moved[half:]


def sums_kernel(near, wanted, c0, c1, a0, a1, w0, w1, *refs):
    half, side = a0.shape[1:]
    place = lax.axis_index("probe")
    strip = (place >= 2) == near
    right = lax.axis_index("tile") == 1
    down = lax.broadcasted_iota(jnp.int32, (half, side), 0) + lax.rem(place, 2) * half
    along = lax.broadcasted_iota(jnp.int32, (half, side), 1)
    zero = jnp.zeros((half, side), jnp.float32)
    here = side_sums = (zero, zero)
    for corner, w, a in ((c0, w0, a0), (c1, w1, a1)):
        corner = corner[...].astype(jnp.float32)
        cy, cx = corner[0:1].astype(jnp.int32), corner[1:2].astype(jnp.int32)
        wave, adjoint = ((x[0].astype(jnp.float32), x[1].astype(jnp.float32)) for x in (w, a))
        inside, own = (down < cy) == strip, (along < cx) == right
        gradient = [jnp.where(inside, x, zero) for x in conj_times(wave, adjoint)]
        here = [total + jnp.where(own, x, zero) for total, x in zip(here, gradient)]
        side_sums = [total + jnp.where(own, zero, x) for total, x in zip(side_sums, gradient)]
    for ref, result in zip(refs, (here, side_sums)[wanted]):
        for part in range(2):
            ref[part] = result[part].astype(ref.dtype)


def copy_kernel(in_ref, *refs):
    refs[-1][...] = in_ref[...]


def early_kernel(out_ref):
    out_ref[...] = jnp.zeros_like(out_ref)


def in_hbm(*arrays):
    return [pltpu.with_memory_space_constraint(x, pltpu.HBM) for x in arrays]


def two_slices(stored_waves, transmission, residual, offsets, slot_position):
    side = stored_waves.shape[-1]
    half = side // 2
    table = jnp.asarray(propagator(side))
    vmem, smem, hbm = (pl.BlockSpec(memory_space=m) for m in (pltpu.VMEM, pltpu.SMEM, pltpu.HBM))
    block, sums = (jax.ShapeDtypeStruct((2, half, side), t) for t in (jnp.bfloat16, jnp.float32))
    params = pltpu.CompilerParams(vmem_limit_bytes=32 * 1024 * 1024)
    by_column = offsets.T
    early = pl.pallas_call(
        early_kernel,
        out_shape=jax.ShapeDtypeStruct((8, 128), jnp.float32),
        out_specs=vmem,
        compiler_params=params,
        cost_estimate=pl.CostEstimate(flops=3 * 10**8, bytes_accessed=0, transcendentals=0),
        name="early",
    )()
    waves, early = lax.optimization_barrier((stored_waves[0, 0], early))
    adj_own, adj_other, corner = pl.pallas_call(
        send_kernel,
        out_shape=(block, block, jax.ShapeDtypeStruct((CORNER_ROWS, side), jnp.bfloat16)),
        in_specs=[vmem, smem, hbm, hbm, vmem, vmem],
        out_specs=(vmem,) * 3,
        scratch_shapes=[
            pltpu.SMEM(by_column.shape, jnp.int32),
            pltpu.VMEM((2, side, side), jnp.bfloat16),
            pltpu.SemaphoreType.DMA((2,)),
        ],
        compiler_params=params,
        name="adjoint",
    )(early, slot_position, *in_hbm(by_column, transmission[0, 0]), table, residual[0])

    probe_count = lax.axis_size("probe")
    swap_tile = [(0, 1), (1, 0)]
    flip = [(2 * z + d, 2 * z + 1 - d) for z in range(probe_count) for d in range(2)]
    flip_z1 = [(2 * z + d, 2 * (z ^ 1) + 1 - d) for z in range(probe_count) for d in range(2)]
    z1, z2 = ([(z, z ^ n) for z in range(probe_count)] for n in (1, 2))
    a_own = lax.ppermute(adj_own, ("probe", "depth"), flip)
    a_next = lax.ppermute(adj_other, ("probe", "depth"), flip_z1)
    w_next = lax.ppermute(waves, "probe", z1)
    corner_next = lax.ppermute(corner, "probe", z1)
    w_own, w_next = pl.pallas_call(
        waves_kernel,
        out_shape=(sums, sums),
        in_specs=[vmem] * 4,
        out_specs=(vmem,) * 2,
        compiler_params=params,
        name="rolled_waves",
    )(corner, corner_next, waves, w_next)
    def masked_sums(near, wanted, *shapes):
        return pl.pallas_call(
            functools.partial(sums_kernel, near, wanted),
            out_shape=shapes,
            in_specs=[vmem] * 6,
            out_specs=(vmem,) * len(shapes),
            compiler_params=params,
            name="near_sums" if near else "far_sums",
        )(corner, corner_next, a_own, a_next, w_own, w_next)

    (side_send,), (send,) = masked_sums(False, slice(1, 2), block), masked_sums(False, slice(0, 1), sums)
    keep, side_keep = masked_sums(True, slice(0, 2), sums, block)
    send = (send + lax.ppermute(side_send, "tile", swap_tile).astype(jnp.float32)).astype(jnp.bfloat16)

    def after(x, *earlier):
        return pl.pallas_call(
            copy_kernel,
            out_shape=jax.ShapeDtypeStruct(x.shape, x.dtype),
            in_specs=[vmem] * (1 + len(earlier)),
            out_specs=vmem,
            compiler_params=params,
            name="after",
        )(x, *earlier)

    odd = lax.axis_index("probe") % 2 == 1
    even_far, odd_far = (
        [(2 * z + t, 2 * (z ^ 2) + t if z % 2 == turn else 2 * z + 1 - t) for z in range(probe_count) for t in range(2)]
        for turn in range(2)
    )
    once = lax.ppermute(after(corner, send), "tile", swap_tile)
    first = lax.ppermute(after(send, side_keep), ("probe", "tile"), even_far)
    twice = lax.ppermute(after(corner, once), "tile", swap_tile)
    near = lax.ppermute(after(side_keep, first), "tile", swap_tile)
    third = lax.ppermute(after(send, twice), ("probe", "tile"), odd_far)
    far = jnp.where(odd, third, first)
    return (keep + (near.astype(jnp.float32) + far.astype(jnp.float32)))[:, None]


def times(a, b, spec):
    return jnp.einsum(spec, a, b, precision=lax.Precision.HIGHEST)


def back_propagate(field):
    side = field.shape[-1]
    real, imag = jnp.asarray(propagator(side))
    for spec in ("kn,pnm->pkm", "mk,pnm->pnk"):
        fr, fi = field[:, 0], field[:, 1]
        field = jnp.stack(
            [times(real, fr, spec) - times(imag, fi, spec), times(real, fi, spec) + times(imag, fr, spec)], 1
        )
    return field


def any_slices(stored_waves, transmission, residual, offsets, slot_position):
    slot_count, side = stored_waves.shape[1], stored_waves.shape[-1]
    depth_count, depth_index = lax.axis_size("depth"), lax.axis_index("depth")
    waves = stored_waves[0].astype(jnp.float32)
    layers = transmission[0].astype(jnp.float32)

    def product(a, b):
        return jnp.stack(conj_times((a[:, 0], a[:, 1]), (b[:, 0], b[:, 1])), 1)

    adjoint = residual
    for turn in range(1, depth_count):
        handed = product(layers, adjoint).astype(jnp.bfloat16)
        got = lax.ppermute(handed, "depth", [(d, d - 1) for d in range(1, depth_count)])
        active = depth_index == depth_count - 1 - turn
        adjoint = lax.cond(active, lambda: back_propagate(got.astype(jnp.float32)), lambda: adjoint)
    gradient = jnp.moveaxis(product(waves, adjoint), 1, 0)
    corners = offsets[slot_position]

    def add_patch(number, region):
        patch = lax.dynamic_index_in_dim(gradient, number, 1, keepdims=True)
        corner = (0, 0, corners[number, 0], corners[number, 1])
        current = lax.dynamic_slice(region, corner, patch.shape)
        return lax.dynamic_update_slice(region, current + patch, corner)

    region = lax.fori_loop(0, slot_count, add_patch, jnp.zeros((2, 1, OBJ, OBJ), jnp.float32))
    strips = lax.psum_scatter(region, "probe", scatter_dimension=2, tiled=True)
    return lax.psum_scatter(strips, "tile", scatter_dimension=3, tiled=True)


def solution(mesh):
    sizes = dict(mesh.shape)

    def per_device(stored_waves, *rest):
        small = (sizes["depth"], sizes["probe"], sizes["tile"], stored_waves.shape[1]) == (2, 4, 2, 1)
        small = small and 2 * stored_waves.shape[-1] == OBJ
        return (two_slices if small else any_slices)(stored_waves, *rest)

    slots = ("groups", "probe", "tile")
    return jax.shard_map(
        per_device,
        mesh=mesh,
        in_specs=(
            P("depth", slots, None, None, None),
            P("depth", slots, None, None, None),
            P(slots, None, None, None),
            P("groups", None),
            P(slots),
        ),
        out_specs=P("groups", "depth", "probe", "tile"),
        check_vma=False,
    )
```

```python
import functools

import jax
import jax.numpy as jnp
import numpy as np
from jax import lax
from jax.experimental import pallas as pl
from jax.experimental.pallas import tpu as pltpu
from jax.sharding import PartitionSpec as P

OBJ = 512
CORNER_ROWS = 16


def propagator(side):
    counter = np.arange(side)
    frequency = (counter + side // 2) % side - side // 2
    chirp = np.exp(0.5j * frequency.astype(np.float64) ** 2 / side)
    ring = np.fft.ifft(chirp)
    ring = 0.5 * (ring + ring[(-counter) % side])
    matrix = ring[(counter[:, None] - counter[None, :]) % side]
    return np.stack([matrix.real, matrix.imag]).astype(np.float32)


def mm(a, b):
    return jnp.dot(a, b, preferred_element_type=jnp.float32)


def split(x):
    high = x.astype(jnp.bfloat16)
    return high, (x - high.astype(jnp.float32)).astype(jnp.bfloat16)


def rolls(side, cy, cx):
    down = lax.broadcasted_iota(jnp.int32, (side, side), 0)
    along = lax.broadcasted_iota(jnp.int32, (side, side), 1)
    rows = (along == ((down - cy) & (side - 1))).astype(jnp.bfloat16)
    cols = (down == ((along - cx) & (side - 1))).astype(jnp.bfloat16)
    return rows, cols


def rolled(parts, rows, cols):
    side = rows.shape[0]
    moved = mm(jnp.concatenate(parts, axis=0), cols).astype(jnp.bfloat16)
    return [mm(rows, moved[n * side : (n + 1) * side]).astype(jnp.bfloat16) for n in range(len(parts))]


def conj_times(a, b):
    return a[0] * b[0] + a[1] * b[1], a[0] * b[1] - a[1] * b[0]


def send_kernel(
    early_ref, slot_ref, offsets_hbm, layer_hbm, table_ref, residual_ref,
    own_ref, other_ref, corner_ref,
    offsets_ref, layer_ref, sems,
):
    side = layer_ref.shape[-1]
    half = side // 2
    del early_ref
    offsets_copy = pltpu.make_async_copy(offsets_hbm, offsets_ref, sems.at[0])
    layer_copy = pltpu.make_async_copy(layer_hbm, layer_ref, sems.at[1])
    offsets_copy.start()
    layer_copy.start()
    offsets_copy.wait()
    slot = slot_ref[0]
    cy, cx = offsets_ref[0, slot], offsets_ref[1, slot]
    parity = lax.rem(lax.axis_index("probe"), 2)
    down = (cy - parity * half) & (side - 1)
    line = lax.broadcasted_iota(jnp.int32, corner_ref.shape, 0)
    corner_ref[...] = jnp.where(line == 0, cy.astype(jnp.float32), cx.astype(jnp.float32)).astype(jnp.bfloat16)
    top = lax.axis_index("depth") == 1

    def put(part, x):
        own_ref[part] = x[:half]
        other_ref[part] = x[half:]

    @pl.when(top)
    def _():
        layer_copy.wait()
        layer = layer_ref[0].astype(jnp.float32), layer_ref[1].astype(jnp.float32)
        handed = conj_times(layer, (residual_ref[0], residual_ref[1]))
        vr, vi = (x.astype(jnp.bfloat16) for x in handed)
        (rhr, rlr), (rhi, rli) = (split(pltpu.roll(table_ref[n], cx, 1)) for n in range(2))
        field = jnp.concatenate([vr, vr, vi, vi], axis=1)
        middle = (
            mm(field, jnp.concatenate([rlr, rhr, -rli, -rhi], axis=0)),
            mm(field, jnp.concatenate([rli, rhi, rlr, rhr], axis=0)),
        )
        (lhr, llr), (lhi, lli) = (split(pltpu.roll(table_ref[n], (side - down) & (side - 1), 1)) for n in range(2))
        (mhr, mlr), (mhi, mli) = map(split, middle)
        field = jnp.concatenate([mlr, mhr, mhr, mli, mhi, mhi], axis=0)
        for part, x in enumerate(([lhr, llr, lhr, -lhi, -lli, -lhi], [lhi, lli, lhi, lhr, llr, lhr])):
            put(part, mm(jnp.concatenate(x, axis=1), field).astype(jnp.bfloat16))

    @pl.when(jnp.logical_not(top))
    def _():
        layer_copy.wait()
        rows, cols = rolls(side, down, cx)
        for part, x in enumerate(rolled([residual_ref[n].astype(jnp.bfloat16) for n in range(2)], rows, cols)):
            put(part, x)


def waves_kernel(c0, c1, w0, w1, near_ref, next_ref):
    side = w0.shape[-1]
    half = side // 2
    parity = lax.rem(lax.axis_index("probe"), 2)
    down = lax.broadcasted_iota(jnp.int32, (half, side), 0) + parity * half
    along = lax.broadcasted_iota(jnp.int32, (half, side), 1)
    every = lax.broadcasted_iota(jnp.int32, (side, side), 0)
    across = lax.broadcasted_iota(jnp.int32, (side, side), 1)
    for corner, w, out in ((c0, w0, near_ref), (c1, w1, next_ref)):
        corner = corner[...].astype(jnp.float32)
        cy, cx = corner[0:1].astype(jnp.int32), corner[1:2].astype(jnp.int32)
        rows = (along == ((down - cy) & (side - 1))).astype(jnp.bfloat16)
        cols = (every == ((across - cx) & (side - 1))).astype(jnp.bfloat16)
        moved = mm(rows, jnp.concatenate([w[0], w[1]], axis=1)).astype(jnp.bfloat16)
        moved = mm(jnp.concatenate([moved[:, :side], moved[:, side:]], axis=0), cols)
        out[0] = moved[:half]
        out[1] = moved[half:]


def sums_kernel(near, wanted, c0, c1, a0, a1, w0, w1, *refs):
    half, side = a0.shape[1:]
    place = lax.axis_index("probe")
    strip = (place >= 2) == near
    right = lax.axis_index("tile") == 1
    down = lax.broadcasted_iota(jnp.int32, (half, side), 0) + lax.rem(place, 2) * half
    along = lax.broadcasted_iota(jnp.int32, (half, side), 1)
    zero = jnp.zeros((half, side), jnp.float32)
    here = side_sums = (zero, zero)
    for corner, w, a in ((c0, w0, a0), (c1, w1, a1)):
        corner = corner[...].astype(jnp.float32)
        cy, cx = corner[0:1].astype(jnp.int32), corner[1:2].astype(jnp.int32)
        wave, adjoint = ((x[0].astype(jnp.float32), x[1].astype(jnp.float32)) for x in (w, a))
        inside, own = (down < cy) == strip, (along < cx) == right
        gradient = [jnp.where(inside, x, zero) for x in conj_times(wave, adjoint)]
        here = [total + jnp.where(own, x, zero) for total, x in zip(here, gradient)]
        side_sums = [total + jnp.where(own, zero, x) for total, x in zip(side_sums, gradient)]
    for ref, result in zip(refs, (here, side_sums)[wanted]):
        for part in range(2):
            ref[part] = result[part].astype(ref.dtype)


def add_kernel(here_ref, side_ref, later_ref, out_ref):
    del later_ref
    out_ref[...] = (here_ref[...] + side_ref[...].astype(jnp.float32)).astype(jnp.bfloat16)


def copy_kernel(in_ref, *refs):
    refs[-1][...] = in_ref[...]


def early_kernel(out_ref):
    out_ref[...] = jnp.zeros_like(out_ref)


def in_hbm(*arrays):
    return [pltpu.with_memory_space_constraint(x, pltpu.HBM) for x in arrays]


def two_slices(stored_waves, transmission, residual, offsets, slot_position):
    side = stored_waves.shape[-1]
    half = side // 2
    table = jnp.asarray(propagator(side))
    vmem, smem, hbm = (pl.BlockSpec(memory_space=m) for m in (pltpu.VMEM, pltpu.SMEM, pltpu.HBM))
    block, sums = (jax.ShapeDtypeStruct((2, half, side), t) for t in (jnp.bfloat16, jnp.float32))
    params = pltpu.CompilerParams(vmem_limit_bytes=32 * 1024 * 1024)
    by_column = offsets.T
    early = pl.pallas_call(
        early_kernel,
        out_shape=jax.ShapeDtypeStruct((8, 128), jnp.float32),
        out_specs=vmem,
        compiler_params=params,
        cost_estimate=pl.CostEstimate(flops=3 * 10**8, bytes_accessed=0, transcendentals=0),
        name="early",
    )()
    waves, early = lax.optimization_barrier((stored_waves[0, 0], early))
    adj_own, adj_other, corner = pl.pallas_call(
        send_kernel,
        out_shape=(block, block, jax.ShapeDtypeStruct((CORNER_ROWS, side), jnp.bfloat16)),
        in_specs=[vmem, smem, hbm, hbm, vmem, vmem],
        out_specs=(vmem,) * 3,
        scratch_shapes=[
            pltpu.SMEM(by_column.shape, jnp.int32),
            pltpu.VMEM((2, side, side), jnp.bfloat16),
            pltpu.SemaphoreType.DMA((2,)),
        ],
        compiler_params=params,
        name="adjoint",
    )(early, slot_position, *in_hbm(by_column, transmission[0, 0]), table, residual[0])

    probe_count = lax.axis_size("probe")
    swap_tile = [(0, 1), (1, 0)]
    flip = [(2 * z + d, 2 * z + 1 - d) for z in range(probe_count) for d in range(2)]
    flip_z1 = [(2 * z + d, 2 * (z ^ 1) + 1 - d) for z in range(probe_count) for d in range(2)]
    z1, z2 = ([(z, z ^ n) for z in range(probe_count)] for n in (1, 2))
    a_own = lax.ppermute(adj_own, ("probe", "depth"), flip)
    a_next = lax.ppermute(adj_other, ("probe", "depth"), flip_z1)
    w_next = lax.ppermute(waves, "probe", z1)
    corner_next = lax.ppermute(corner, "probe", z1)
    w_own, w_next = pl.pallas_call(
        waves_kernel,
        out_shape=(sums, sums),
        in_specs=[vmem] * 4,
        out_specs=(vmem,) * 2,
        compiler_params=params,
        name="rolled_waves",
    )(corner, corner_next, waves, w_next)
    def masked_sums(near, wanted, *shapes):
        return pl.pallas_call(
            functools.partial(sums_kernel, near, wanted),
            out_shape=shapes,
            in_specs=[vmem] * 6,
            out_specs=(vmem,) * len(shapes),
            compiler_params=params,
            name="near_sums" if near else "far_sums",
        )(corner, corner_next, a_own, a_next, w_own, w_next)

    (side_send,), (send,) = masked_sums(False, slice(1, 2), block), masked_sums(False, slice(0, 1), sums)
    keep, side_keep = masked_sums(True, slice(0, 2), sums, block)
    send = pl.pallas_call(
        add_kernel,
        out_shape=block,
        in_specs=[vmem] * 3,
        out_specs=vmem,
        compiler_params=params,
        name="far_total",
    )(send, lax.ppermute(side_send, "tile", swap_tile), side_keep)

    def after(x, *earlier):
        return pl.pallas_call(
            copy_kernel,
            out_shape=jax.ShapeDtypeStruct(x.shape, x.dtype),
            in_specs=[vmem] * (1 + len(earlier)),
            out_specs=vmem,
            compiler_params=params,
            name="after",
        )(x, *earlier)

    odd = lax.axis_index("probe") % 2 == 1
    even_far, odd_far = (
        [(2 * z + t, 2 * (z ^ 2) + t if z % 2 == turn else 2 * z + 1 - t) for z in range(probe_count) for t in range(2)]
        for turn in range(2)
    )
    once = lax.ppermute(after(corner, send), "tile", swap_tile)
    first = lax.ppermute(send, ("probe", "tile"), even_far)
    twice = lax.ppermute(after(corner, once), "tile", swap_tile)
    near = lax.ppermute(after(side_keep, first), "tile", swap_tile)
    third = lax.ppermute(after(send, twice), ("probe", "tile"), odd_far)
    far = jnp.where(odd, third, first)
    return (keep + (near.astype(jnp.float32) + far.astype(jnp.float32)))[:, None]


def times(a, b, spec):
    return jnp.einsum(spec, a, b, precision=lax.Precision.HIGHEST)


def back_propagate(field):
    side = field.shape[-1]
    real, imag = jnp.asarray(propagator(side))
    for spec in ("kn,pnm->pkm", "mk,pnm->pnk"):
        fr, fi = field[:, 0], field[:, 1]
        field = jnp.stack(
            [times(real, fr, spec) - times(imag, fi, spec), times(real, fi, spec) + times(imag, fr, spec)], 1
        )
    return field


def any_slices(stored_waves, transmission, residual, offsets, slot_position):
    slot_count, side = stored_waves.shape[1], stored_waves.shape[-1]
    depth_count, depth_index = lax.axis_size("depth"), lax.axis_index("depth")
    waves = stored_waves[0].astype(jnp.float32)
    layers = transmission[0].astype(jnp.float32)

    def product(a, b):
        return jnp.stack(conj_times((a[:, 0], a[:, 1]), (b[:, 0], b[:, 1])), 1)

    adjoint = residual
    for turn in range(1, depth_count):
        handed = product(layers, adjoint).astype(jnp.bfloat16)
        got = lax.ppermute(handed, "depth", [(d, d - 1) for d in range(1, depth_count)])
        active = depth_index == depth_count - 1 - turn
        adjoint = lax.cond(active, lambda: back_propagate(got.astype(jnp.float32)), lambda: adjoint)
    gradient = jnp.moveaxis(product(waves, adjoint), 1, 0)
    corners = offsets[slot_position]

    def add_patch(number, region):
        patch = lax.dynamic_index_in_dim(gradient, number, 1, keepdims=True)
        corner = (0, 0, corners[number, 0], corners[number, 1])
        current = lax.dynamic_slice(region, corner, patch.shape)
        return lax.dynamic_update_slice(region, current + patch, corner)

    region = lax.fori_loop(0, slot_count, add_patch, jnp.zeros((2, 1, OBJ, OBJ), jnp.float32))
    strips = lax.psum_scatter(region, "probe", scatter_dimension=2, tiled=True)
    return lax.psum_scatter(strips, "tile", scatter_dimension=3, tiled=True)


def solution(mesh):
    sizes = dict(mesh.shape)

    def per_device(stored_waves, *rest):
        small = (sizes["depth"], sizes["probe"], sizes["tile"], stored_waves.shape[1]) == (2, 4, 2, 1)
        small = small and 2 * stored_waves.shape[-1] == OBJ
        return (two_slices if small else any_slices)(stored_waves, *rest)

    slots = ("groups", "probe", "tile")
    return jax.shard_map(
        per_device,
        mesh=mesh,
        in_specs=(
            P("depth", slots, None, None, None),
            P("depth", slots, None, None, None),
            P(slots, None, None, None),
            P("groups", None),
            P(slots),
        ),
        out_specs=P("groups", "depth", "probe", "tile"),
        check_vma=False,
    )
```

```python
import functools

import jax
import jax.numpy as jnp
import numpy as np
from jax import lax
from jax.experimental import pallas as pl
from jax.experimental.pallas import tpu as pltpu
from jax.sharding import PartitionSpec as P

OBJ = 512
CORNER_ROWS = 16


def propagator(side):
    counter = np.arange(side)
    frequency = (counter + side // 2) % side - side // 2
    chirp = np.exp(0.5j * frequency.astype(np.float64) ** 2 / side)
    ring = np.fft.ifft(chirp)
    ring = 0.5 * (ring + ring[(-counter) % side])
    matrix = ring[(counter[:, None] - counter[None, :]) % side]
    return np.stack([matrix.real, matrix.imag]).astype(np.float32)


def mm(a, b):
    return jnp.dot(a, b, preferred_element_type=jnp.float32)


def split(x):
    high = x.astype(jnp.bfloat16)
    return high, (x - high.astype(jnp.float32)).astype(jnp.bfloat16)


def rolls(side, cy, cx):
    down = lax.broadcasted_iota(jnp.int32, (side, side), 0)
    along = lax.broadcasted_iota(jnp.int32, (side, side), 1)
    rows = (along == ((down - cy) & (side - 1))).astype(jnp.bfloat16)
    cols = (down == ((along - cx) & (side - 1))).astype(jnp.bfloat16)
    return rows, cols


def rolled(parts, rows, cols):
    side = rows.shape[0]
    moved = mm(jnp.concatenate(parts, axis=0), cols).astype(jnp.bfloat16)
    return [mm(rows, moved[n * side : (n + 1) * side]).astype(jnp.bfloat16) for n in range(len(parts))]


def conj_times(a, b):
    return a[0] * b[0] + a[1] * b[1], a[0] * b[1] - a[1] * b[0]


def send_kernel(
    early_ref, slot_ref, offsets_hbm, layer_hbm, table_ref, residual_ref,
    own_ref, other_ref, corner_ref,
    offsets_ref, layer_ref, sems,
):
    side = layer_ref.shape[-1]
    half = side // 2
    del early_ref
    offsets_copy = pltpu.make_async_copy(offsets_hbm, offsets_ref, sems.at[0])
    layer_copies = [pltpu.make_async_copy(layer_hbm.at[n], layer_ref.at[n], sems.at[1 + n]) for n in range(2)]
    offsets_copy.start()
    for copy in layer_copies:
        copy.start()
    offsets_copy.wait()
    slot = slot_ref[0]
    cy, cx = offsets_ref[0, slot], offsets_ref[1, slot]
    parity = lax.rem(lax.axis_index("probe"), 2)
    down = (cy - parity * half) & (side - 1)
    line = lax.broadcasted_iota(jnp.int32, corner_ref.shape, 0)
    corner_ref[...] = jnp.where(line == 0, cy.astype(jnp.float32), cx.astype(jnp.float32)).astype(jnp.bfloat16)
    top = lax.axis_index("depth") == 1

    def put(part, x):
        own_ref[part] = x[:half]
        other_ref[part] = x[half:]

    @pl.when(top)
    def _():
        for copy in layer_copies:
            copy.wait()
        layer = layer_ref[0].astype(jnp.float32), layer_ref[1].astype(jnp.float32)
        handed = conj_times(layer, (residual_ref[0], residual_ref[1]))
        vr, vi = (x.astype(jnp.bfloat16) for x in handed)
        (rhr, rlr), (rhi, rli) = (split(pltpu.roll(table_ref[n], cx, 1)) for n in range(2))
        field = jnp.concatenate([vr, vr, vi, vi], axis=1)
        middle = (
            mm(field, jnp.concatenate([rlr, rhr, -rli, -rhi], axis=0)),
            mm(field, jnp.concatenate([rli, rhi, rlr, rhr], axis=0)),
        )
        (lhr, llr), (lhi, lli) = (split(pltpu.roll(table_ref[n], (side - down) & (side - 1), 1)) for n in range(2))
        (mhr, mlr), (mhi, mli) = map(split, middle)
        field = jnp.concatenate([mlr, mhr, mhr, mli, mhi, mhi], axis=0)
        for part, x in enumerate(([lhr, llr, lhr, -lhi, -lli, -lhi], [lhi, lli, lhi, lhr, llr, lhr])):
            put(part, mm(jnp.concatenate(x, axis=1), field).astype(jnp.bfloat16))

    @pl.when(jnp.logical_not(top))
    def _():
        for copy in layer_copies:
            copy.wait()
        rows, cols = rolls(side, down, cx)
        for part, x in enumerate(rolled([residual_ref[n].astype(jnp.bfloat16) for n in range(2)], rows, cols)):
            put(part, x)


def waves_kernel(c0, c1, w0, w1, near_ref, next_ref):
    side = w0.shape[-1]
    half = side // 2
    parity = lax.rem(lax.axis_index("probe"), 2)
    down = lax.broadcasted_iota(jnp.int32, (half, side), 0) + parity * half
    along = lax.broadcasted_iota(jnp.int32, (half, side), 1)
    every = lax.broadcasted_iota(jnp.int32, (side, side), 0)
    across = lax.broadcasted_iota(jnp.int32, (side, side), 1)
    for corner, w, out in ((c0, w0, near_ref), (c1, w1, next_ref)):
        corner = corner[...].astype(jnp.float32)
        cy, cx = corner[0:1].astype(jnp.int32), corner[1:2].astype(jnp.int32)
        rows = (along == ((down - cy) & (side - 1))).astype(jnp.bfloat16)
        cols = (every == ((across - cx) & (side - 1))).astype(jnp.bfloat16)
        moved = mm(rows, jnp.concatenate([w[0], w[1]], axis=1)).astype(jnp.bfloat16)
        moved = mm(jnp.concatenate([moved[:, :side], moved[:, side:]], axis=0), cols)
        out[0] = moved[:half]
        out[1] = moved[half:]


def sums_kernel(near, wanted, c0, c1, a0, a1, w0, w1, *refs):
    half, side = a0.shape[1:]
    place = lax.axis_index("probe")
    strip = (place >= 2) == near
    right = lax.axis_index("tile") == 1
    down = lax.broadcasted_iota(jnp.int32, (half, side), 0) + lax.rem(place, 2) * half
    along = lax.broadcasted_iota(jnp.int32, (half, side), 1)
    zero = jnp.zeros((half, side), jnp.float32)
    here = side_sums = (zero, zero)
    for corner, w, a in ((c0, w0, a0), (c1, w1, a1)):
        corner = corner[...].astype(jnp.float32)
        cy, cx = corner[0:1].astype(jnp.int32), corner[1:2].astype(jnp.int32)
        wave, adjoint = ((x[0].astype(jnp.float32), x[1].astype(jnp.float32)) for x in (w, a))
        inside, own = (down < cy) == strip, (along < cx) == right
        gradient = [jnp.where(inside, x, zero) for x in conj_times(wave, adjoint)]
        here = [total + jnp.where(own, x, zero) for total, x in zip(here, gradient)]
        side_sums = [total + jnp.where(own, zero, x) for total, x in zip(side_sums, gradient)]
    for ref, result in zip(refs, (here, side_sums)[wanted]):
        for part in range(2):
            ref[part] = result[part].astype(ref.dtype)


def add_kernel(here_ref, side_ref, later_ref, out_ref):
    del later_ref
    out_ref[...] = (here_ref[...] + side_ref[...].astype(jnp.float32)).astype(jnp.bfloat16)


def copy_kernel(in_ref, *refs):
    refs[-1][...] = in_ref[...]


def early_kernel(out_ref):
    out_ref[...] = jnp.zeros_like(out_ref)


def in_hbm(*arrays):
    return [pltpu.with_memory_space_constraint(x, pltpu.HBM) for x in arrays]


def two_slices(stored_waves, transmission, residual, offsets, slot_position):
    side = stored_waves.shape[-1]
    half = side // 2
    table = jnp.asarray(propagator(side))
    vmem, smem, hbm = (pl.BlockSpec(memory_space=m) for m in (pltpu.VMEM, pltpu.SMEM, pltpu.HBM))
    block, sums = (jax.ShapeDtypeStruct((2, half, side), t) for t in (jnp.bfloat16, jnp.float32))
    params = pltpu.CompilerParams(vmem_limit_bytes=32 * 1024 * 1024)
    by_column = offsets.T
    early = pl.pallas_call(
        early_kernel,
        out_shape=jax.ShapeDtypeStruct((8, 128), jnp.float32),
        out_specs=vmem,
        compiler_params=params,
        cost_estimate=pl.CostEstimate(flops=3 * 10**8, bytes_accessed=0, transcendentals=0),
        name="early",
    )()
    waves, early = lax.optimization_barrier((stored_waves[0, 0], early))
    adj_own, adj_other, corner = pl.pallas_call(
        send_kernel,
        out_shape=(block, block, jax.ShapeDtypeStruct((CORNER_ROWS, side), jnp.bfloat16)),
        in_specs=[vmem, smem, hbm, hbm, vmem, vmem],
        out_specs=(vmem,) * 3,
        scratch_shapes=[
            pltpu.SMEM(by_column.shape, jnp.int32),
            pltpu.VMEM((2, side, side), jnp.bfloat16),
            pltpu.SemaphoreType.DMA((3,)),
        ],
        compiler_params=params,
        name="adjoint",
    )(early, slot_position, *in_hbm(by_column, transmission[0, 0]), table, residual[0])

    probe_count = lax.axis_size("probe")
    swap_tile = [(0, 1), (1, 0)]
    flip = [(2 * z + d, 2 * z + 1 - d) for z in range(probe_count) for d in range(2)]
    flip_z1 = [(2 * z + d, 2 * (z ^ 1) + 1 - d) for z in range(probe_count) for d in range(2)]
    z1, z2 = ([(z, z ^ n) for z in range(probe_count)] for n in (1, 2))
    a_own = lax.ppermute(adj_own, ("probe", "depth"), flip)
    a_next = lax.ppermute(adj_other, ("probe", "depth"), flip_z1)
    w_next = lax.ppermute(waves, "probe", z1)
    corner_next = lax.ppermute(corner, "probe", z1)
    w_own, w_next = pl.pallas_call(
        waves_kernel,
        out_shape=(sums, sums),
        in_specs=[vmem] * 4,
        out_specs=(vmem,) * 2,
        compiler_params=params,
        name="rolled_waves",
    )(corner, corner_next, waves, w_next)
    def masked_sums(near, wanted, *shapes):
        return pl.pallas_call(
            functools.partial(sums_kernel, near, wanted),
            out_shape=shapes,
            in_specs=[vmem] * 6,
            out_specs=(vmem,) * len(shapes),
            compiler_params=params,
            name="near_sums" if near else "far_sums",
        )(corner, corner_next, a_own, a_next, w_own, w_next)

    (side_send,), (send,) = masked_sums(False, slice(1, 2), block), masked_sums(False, slice(0, 1), sums)
    keep, side_keep = masked_sums(True, slice(0, 2), sums, block)
    send = pl.pallas_call(
        add_kernel,
        out_shape=block,
        in_specs=[vmem] * 3,
        out_specs=vmem,
        compiler_params=params,
        name="far_total",
    )(send, lax.ppermute(side_send, "tile", swap_tile), side_keep)

    def after(x, *earlier):
        return pl.pallas_call(
            copy_kernel,
            out_shape=jax.ShapeDtypeStruct(x.shape, x.dtype),
            in_specs=[vmem] * (1 + len(earlier)),
            out_specs=vmem,
            compiler_params=params,
            name="after",
        )(x, *earlier)

    odd = lax.axis_index("probe") % 2 == 1
    even_far, odd_far = (
        [(2 * z + t, 2 * (z ^ 2) + t if z % 2 == turn else 2 * z + 1 - t) for z in range(probe_count) for t in range(2)]
        for turn in range(2)
    )
    once = lax.ppermute(after(corner, send), "tile", swap_tile)
    first = lax.ppermute(send, ("probe", "tile"), even_far)
    twice = lax.ppermute(after(corner, once), "tile", swap_tile)
    near = lax.ppermute(after(side_keep, first), "tile", swap_tile)
    third = lax.ppermute(after(send, twice), ("probe", "tile"), odd_far)
    far = jnp.where(odd, third, first)
    return (keep + (near.astype(jnp.float32) + far.astype(jnp.float32)))[:, None]


def times(a, b, spec):
    return jnp.einsum(spec, a, b, precision=lax.Precision.HIGHEST)


def back_propagate(field):
    side = field.shape[-1]
    real, imag = jnp.asarray(propagator(side))
    for spec in ("kn,pnm->pkm", "mk,pnm->pnk"):
        fr, fi = field[:, 0], field[:, 1]
        field = jnp.stack(
            [times(real, fr, spec) - times(imag, fi, spec), times(real, fi, spec) + times(imag, fr, spec)], 1
        )
    return field


def any_slices(stored_waves, transmission, residual, offsets, slot_position):
    slot_count, side = stored_waves.shape[1], stored_waves.shape[-1]
    depth_count, depth_index = lax.axis_size("depth"), lax.axis_index("depth")
    waves = stored_waves[0].astype(jnp.float32)
    layers = transmission[0].astype(jnp.float32)

    def product(a, b):
        return jnp.stack(conj_times((a[:, 0], a[:, 1]), (b[:, 0], b[:, 1])), 1)

    adjoint = residual
    for turn in range(1, depth_count):
        handed = product(layers, adjoint).astype(jnp.bfloat16)
        got = lax.ppermute(handed, "depth", [(d, d - 1) for d in range(1, depth_count)])
        active = depth_index == depth_count - 1 - turn
        adjoint = lax.cond(active, lambda: back_propagate(got.astype(jnp.float32)), lambda: adjoint)
    gradient = jnp.moveaxis(product(waves, adjoint), 1, 0)
    corners = offsets[slot_position]

    def add_patch(number, region):
        patch = lax.dynamic_index_in_dim(gradient, number, 1, keepdims=True)
        corner = (0, 0, corners[number, 0], corners[number, 1])
        current = lax.dynamic_slice(region, corner, patch.shape)
        return lax.dynamic_update_slice(region, current + patch, corner)

    region = lax.fori_loop(0, slot_count, add_patch, jnp.zeros((2, 1, OBJ, OBJ), jnp.float32))
    strips = lax.psum_scatter(region, "probe", scatter_dimension=2, tiled=True)
    return lax.psum_scatter(strips, "tile", scatter_dimension=3, tiled=True)


def solution(mesh):
    sizes = dict(mesh.shape)

    def per_device(stored_waves, *rest):
        small = (sizes["depth"], sizes["probe"], sizes["tile"], stored_waves.shape[1]) == (2, 4, 2, 1)
        small = small and 2 * stored_waves.shape[-1] == OBJ
        return (two_slices if small else any_slices)(stored_waves, *rest)

    slots = ("groups", "probe", "tile")
    return jax.shard_map(
        per_device,
        mesh=mesh,
        in_specs=(
            P("depth", slots, None, None, None),
            P("depth", slots, None, None, None),
            P(slots, None, None, None),
            P("groups", None),
            P(slots),
        ),
        out_specs=P("groups", "depth", "probe", "tile"),
        check_vma=False,
    )
```
